256 devices in a mesh: seq: 64 (over z, y, core), chan: 4 (over x).
Axes of the slice: x: 4, y: 4, z: 8, core: 2. Of those that a mesh axis runs over, the one named last changes fastest.
Arguments:
- residual: bfloat16 [8192, 8192], P('seq', 'chan'), may hold values from -6 to 6
- hyena_q: bfloat16 [8192, 8192], P('seq', 'chan'), may hold values from -6 to 6
- hyena_k: bfloat16 [8192, 8192], P('seq', 'chan'), may hold values from -6 to 6
- hyena_v: bfloat16 [8192, 8192], P('seq', 'chan'), may hold values from -6 to 6
- modal_residue: float32 [8192, 16], P('chan'), may hold values from -0.06 to 0.06
- decay_rate: float32 [8192, 16], P('chan'), may hold values from 6.1035156e-05 to 0.05
- skip_gain: float32 [8192], P('chan'), may hold values from -1 to 1
- attn_q: bfloat16 [8192, 8192], P('seq', 'chan'), may hold values from -6 to 6
- attn_k: bfloat16 [8192, 8192], P('seq', 'chan'), may hold values from -6 to 6
- norm_gain: float32 [8192], P('chan'), may hold values from 0.5 to 1.5
- readers: int32 [64, 64], P('seq'), may hold values from -1 to 7, as said below
Outputs:
- block_out: bfloat16 [8192, 8192], P('seq', 'chan')
The draws below stay inside these ranges and needn't reach their ends.
Inputs may be any that keep to these rules, and one draw needn't show every extreme that they name: readers[q, j] is -1 whenever j >= q; otherwise -1 or a tile index below 8.
All inputs are finite; a program needn't handle non-finite values.
Results may differ from the reference program's by a relative error of at most 0.0052.
Values may be sent and summed in bfloat16 or wider, within the bound.
A program may use at most 256 MiB of HBM per device.

```python
import math
import jax
import jax.numpy as jnp
from jax import lax

D = 8192
HEADS = 64
HEAD_DIM = 128
MODES = 16
TILE = 16
TOK_DEV = 128
TOKENS = 8192
NSHARD = 64
TILES = 8


def draw_readers(key, part):
    key = jax.random.fold_in(key, 7)
    first, second = jax.random.split(key)
    tiles = jax.random.randint(first, (NSHARD, NSHARD), 0, TILES)
    kept = jax.random.randint(second, (NSHARD, NSHARD), 0, 4) > 0
    reader_pos = jnp.arange(NSHARD)[:, None]
    source_pos = jnp.arange(NSHARD)[None, :]
    result = jnp.where(kept & (source_pos < reader_pos), tiles, -1)
    result = result.at[NSHARD - 1, 0].set(TILES - 1)
    return result.astype(jnp.int32)


def aligned_layout(key):
    place_key = jax.random.fold_in(key, 101)
    sign_key = jax.random.fold_in(key, 102)
    half_rows = TOK_DEV // 2
    shuffled = jax.vmap(lambda sub_key: jax.random.permutation(sub_key, half_rows))(jax.random.split(place_key, NSHARD))
    shard_starts = (jnp.arange(NSHARD) * TOK_DEV)[:, None]
    query_rows = (shard_starts + half_rows + shuffled[:, 0:3]).reshape(-1).astype(jnp.int32)
    first_keys = (shard_starts + shuffled[:, 3:6]).reshape(-1).astype(jnp.int32)
    second_keys = (shard_starts + shuffled[:, 6:9]).reshape(-1).astype(jnp.int32)
    sign_rows = jnp.where(jax.random.bernoulli(sign_key, 0.5, (NSHARD * 3, D)), 1.0, -1.0).astype(jnp.float32)
    kept_cols = jnp.arange(D) % 16 != 0
    return (query_rows, first_keys, second_keys, sign_rows, kept_cols)


def place_rows(field, rows, sign_rows, kept_cols, amplitudes, masked_fill):
    levels = jnp.tile(jnp.array(amplitudes, jnp.float32), NSHARD)[:, None]
    filler = field[rows] * masked_fill
    aligned = jnp.where(kept_cols[None, :], sign_rows * levels, filler)
    return field.at[rows].set(aligned)


def draw_attn_q(key, part):
    query_rows, first_keys, second_keys, sign_rows, kept_cols = aligned_layout(key)
    key = jax.random.fold_in(key, 11)
    noise_key = jax.random.fold_in(key, 0)
    field = jax.random.truncated_normal(noise_key, -6.0, 6.0, (TOKENS, D))
    amplitudes = (3.25, 4.0, 5.0)
    field = field.astype(jnp.float32)
    return place_rows(field, query_rows, sign_rows, kept_cols, amplitudes, 0.0).astype(jnp.bfloat16)


def draw_attn_k(key, part):
    query_rows, first_keys, second_keys, sign_rows, kept_cols = aligned_layout(key)
    key = jax.random.fold_in(key, 13)
    noise_key = jax.random.fold_in(key, 0)
    field = jax.random.truncated_normal(noise_key, -6.0, 6.0, (TOKENS, D))
    upper = (3.25, 4.0, 5.0)
    lower = (3.1875, 3.953125, 4.96875)
    field = field.astype(jnp.float32)
    field = place_rows(field, first_keys, sign_rows, kept_cols, upper, 1.0)
    return place_rows(field, second_keys, sign_rows, kept_cols, lower, 1.0).astype(jnp.bfloat16)


def shard_levels(key, extent, cuts, least, top_value):
    loudness, own = 1.0, jax.random.fold_in(key, 6)
    for dim, blocks in cuts:
        steps = jnp.exp(jax.random.uniform(jax.random.fold_in(own, dim), (blocks,), jnp.float32, least / len(cuts), top_value / len(cuts)))
        loudness = loudness * jnp.repeat(steps, extent[dim] // blocks).reshape([-1 if axis == dim else 1 for axis in range(len(extent))])
    return loudness


def bell_draw(key, dims, deviation, bound, shards=(), kind=jnp.bfloat16):
    values = jax.random.normal(key, dims, jnp.float32) * deviation
    if len(shards) > 0:
        values = shard_levels(key, dims, shards, -0.22, 0.18) * values
    return jnp.clip(values, min=-bound, max=bound).astype(kind)


def setup_inputs(seed: int = 0) -> dict:
    key_of = jax.random.split(jax.random.key(seed), 12)
    return {
        "residual": bell_draw(key_of[0], (TOKENS, D), 1.0, 6.0, ((0, 64), (1, 4))),
        "hyena_q": bell_draw(key_of[1], (TOKENS, D), 1.0, 6.0, ((0, 64), (1, 4))),
        "hyena_k": bell_draw(key_of[2], (TOKENS, D), 1.0, 6.0, ((0, 64), (1, 4))),
        "hyena_v": bell_draw(key_of[3], (TOKENS, D), 1.0, 6.0, ((0, 64), (1, 4))),
        "modal_residue": bell_draw(key_of[4], (D, MODES), 0.01, 0.06, ((0, 4),), jnp.float32),
        "decay_rate": jnp.clip(jnp.exp(math.log(0.05) - 6.7083283 * jax.random.uniform(key_of[5], (D, MODES), jnp.float32) ** shard_levels(key_of[5], (D, MODES), ((0, 4),), -0.2, 0.2)), 6.103515625e-05, 0.05),
        "skip_gain": jnp.clip(jax.random.uniform(key_of[6], (D,), jnp.float32, -1.0, 1.0) * shard_levels(key_of[6], (D,), ((0, 4),), -0.4, 0.0), -1.0, 1.0),
        "attn_q": draw_attn_q(jax.random.fold_in(key_of[11], 71), 0),
        "attn_k": draw_attn_k(jax.random.fold_in(key_of[11], 71), 0),
        "norm_gain": jnp.clip(1.0 + 0.1 * jax.random.normal(key_of[9], (D,), jnp.float32), 0.5, 1.5),
        "readers": draw_readers(jax.random.fold_in(key_of[11], 71), 0),
    }


def filter_group(operands):
    signal, residue, rates = operands
    length = signal.shape[0]
    steps = jnp.arange(length).astype(signal.dtype)
    kernel = jnp.einsum('gm,gmt->gt', residue, jnp.exp(-rates[:, :, None] * steps), precision=lax.Precision.HIGHEST)
    spectrum = jnp.fft.rfft(signal.T, n=2 * length) * jnp.fft.rfft(kernel, n=2 * length)
    return jnp.fft.irfft(spectrum, n=2 * length)[:, :length].T

def shard_attention(index, stream, values, attn_q, attn_k, readers):
    rows = lax.dynamic_slice_in_dim(attn_q, index * TOK_DEV, TOK_DEV, 0)
    own_keys = lax.dynamic_slice_in_dim(attn_k, index * TOK_DEV, TOK_DEV, 0)
    own_values = lax.dynamic_slice_in_dim(values, index * TOK_DEV, TOK_DEV, 0)
    wanted = readers[index]
    picks = (jnp.arange(NSHARD)[:, None] * TOK_DEV + jnp.clip(wanted, 0)[:, None] * TILE + jnp.arange(TILE)[None, :]).reshape(-1).astype(jnp.int32)
    keys = jnp.concatenate([own_keys, attn_k[picks]], axis=0)
    vals = jnp.concatenate([own_values, values[picks]], axis=0)
    causal = jnp.tril(jnp.ones((TOK_DEV, TOK_DEV), bool))
    remote = jnp.broadcast_to(jnp.repeat(wanted >= 0, TILE)[None, :], (TOK_DEV, NSHARD * TILE))
    allowed = jnp.concatenate([causal, remote], axis=1)
    query_heads = rows.astype(jnp.float32).reshape(TOK_DEV, HEADS, HEAD_DIM)
    key_heads = keys.astype(jnp.float32).reshape(-1, HEADS, HEAD_DIM)
    value_heads = vals.astype(jnp.float32).reshape(-1, HEADS, HEAD_DIM)
    scores = jnp.einsum('qhd,khd->hqk', query_heads, key_heads) / jnp.sqrt(jnp.float32(HEAD_DIM))
    scores = jnp.where(allowed[None], scores, -1e+30)
    peak = lax.optimization_barrier(jnp.max(scores, axis=2, keepdims=True))
    weights = jnp.where(allowed[None], jnp.exp(scores - peak), 0.0)
    total = lax.optimization_barrier(jnp.sum(weights, axis=2))
    rounded = lax.optimization_barrier(weights.astype(jnp.bfloat16)).astype(jnp.float32)
    summed = jnp.einsum('hqk,khd->qhd', rounded, value_heads)
    attended = (summed / total.T[:, :, None]).reshape(TOK_DEV, D)
    own_stream = lax.dynamic_slice_in_dim(stream, index * TOK_DEV, TOK_DEV, 0)
    return (own_stream + attended).astype(jnp.bfloat16)

def reference(residual, hyena_q, hyena_k, hyena_v, modal_residue, decay_rate, skip_gain, attn_q, attn_k, norm_gain, readers):
    product = (hyena_k.astype(jnp.float32) * hyena_v.astype(jnp.float32)).astype(jnp.bfloat16)
    product32 = product.astype(jnp.float32)
    width = min(D, 64)
    groups = D // width
    stacked = product32.reshape(TOKENS, groups, width).transpose(1, 0, 2)
    filtered = lax.map(filter_group, (stacked, modal_residue.reshape(groups, width, MODES), decay_rate.reshape(groups, width, MODES)))
    filtered = filtered.transpose(1, 0, 2).reshape(TOKENS, D)
    convolved = (filtered + skip_gain[None, :] * product32).astype(jnp.bfloat16)
    stream = residual.astype(jnp.float32) + hyena_q.astype(jnp.float32) * convolved.astype(jnp.float32)
    scale_rows = lax.rsqrt(lax.optimization_barrier(jnp.mean(stream * stream, axis=1, keepdims=True)) + 1e-06)
    values = (stream * scale_rows * norm_gain[None, :]).astype(jnp.bfloat16)
    outputs = lax.map(lambda index: shard_attention(index, stream, values, attn_q, attn_k, readers), jnp.arange(NSHARD))
    return outputs.reshape(TOKENS, D)
```

```python
import functools

import jax
import jax.numpy as jnp
from jax import lax
from jax.experimental import pallas as pl
from jax.experimental.pallas import tpu as pltpu
from jax.sharding import PartitionSpec as P

MESH = pl.DeviceIdType.MESH
LANES = 128
TILE = 16
GROUP = 4
F32 = jnp.float32
BF16 = jnp.bfloat16


def remote(src, dst, send, recv, **where):
    return pltpu.make_async_remote_copy(
        src_ref=src,
        dst_ref=dst,
        send_sem=send,
        recv_sem=recv,
        device_id=where,
        device_id_type=MESH,
    )


def drain(ref, sem):
    pltpu.make_async_copy(ref, ref, sem).wait()


def kernel(
    shards,
    planes,
    modes,
    residual,
    hyena_q,
    hyena_k,
    hyena_v,
    residue_ref,
    rate_ref,
    skip_ref,
    attn_q,
    attn_k,
    gain_ref,
    readers,
    out,
    hk,
    hv,
    hq,
    res,
    decay,
    xs,
    ys,
    ends,
    st_in,
    st_out,
    start,
    stream,
    sq,
    vloc,
    q_all,
    k_all,
    v_all,
    rd_all,
    rd_smem,
    tiles,
    weights,
    totals,
    o_stage,
    o_recv,
    out_v,
    load_sem,
    st_send,
    st_recv,
    back_send,
    back_recv,
    sq_send,
    sq_recv,
    rd_send,
    rd_recv,
    q_send,
    q_recv,
    k_send,
    k_recv,
    v_send,
    v_recv,
    kf_send,
    vf_send,
    o_send,
    o_recv_sem,
    out_sem,
):
    me = lax.axis_index("seq")
    plane = lax.axis_index("chan")
    heads = shards // GROUP
    mine = me // GROUP
    rank = me % GROUP
    core_peer = me + 1 - 2 * (me % 2)
    chip_peer = me + 2 - 4 * ((me // 2) % 2)
    core_rank = core_peer % GROUP
    chip_rank = chip_peer % GROUP
    far_rank = (GROUP - 1) - rank
    rows = hk.shape[0]
    ltiles = hk.shape[1] // LANES

    loads = [
        pltpu.make_async_copy(src, dst, load_sem.at[n])
        for n, (src, dst) in enumerate(
            ((hyena_k, hk), (hyena_v, hv), (hyena_q, hq), (residual, res))
        )
    ]
    for load in loads:
        load.start()

    barrier = pltpu.get_barrier_semaphore()

    @pl.loop(1, shards)
    def _(d):
        pl.semaphore_signal(
            barrier, inc=1, device_id={"seq": (me + d) % shards}, device_id_type=MESH
        )

    for d in range(1, planes):
        pl.semaphore_signal(
            barrier, inc=1, device_id={"chan": (plane + d) % planes}, device_id_type=MESH
        )

    decay[...] = jnp.exp(-rate_ref[...])
    loads[0].wait()
    loads[1].wait()

    @pl.loop(0, ltiles)
    def _(lt):
        cols = pl.ds(pl.multiple_of(lt * LANES, LANES), LANES)
        product = (hk[:, cols].astype(F32) * hv[:, cols].astype(F32)).astype(BF16)
        xs[pl.ds(pl.multiple_of(lt * rows, rows), rows), :] = product.astype(F32)

    halves = ltiles // 8
    for half in range(halves):
        part = slice(half * 8, half * 8 + 8)
        base = half * 8 * rows

        def advance(t, states):
            x = xs[pl.ds(base + t, 8, stride=rows), :]
            return tuple(decay[m, part, :] * states[m] + x for m in range(modes))

        states = lax.fori_loop(
            0, rows, advance, tuple(jnp.zeros((8, LANES), F32) for _ in range(modes)), unroll=4
        )
        for m in range(modes):
            slot = (m * ltiles + half * 8) // 4
            ends[slot] = states[m][0:4]
            ends[slot + 1] = states[m][4:8]

    pl.semaphore_wait(barrier, shards - 1 + planes - 1)

    @pl.loop(1, shards)
    def _(d):
        to = (me + d) % shards
        remote(ends.at[to], st_in.at[me], st_send, st_recv, seq=to).start()

    st_in[me] = ends[me]
    blocks_per_mode = ltiles // 4
    my_mode = me // blocks_per_mode
    my_rows = me % blocks_per_mode

    own_cols = pl.ds(pl.multiple_of(mine * LANES, LANES), LANES)
    own_q = pltpu.make_async_copy(attn_q.at[:, :, own_cols], q_all.at[mine], load_sem.at[4])
    own_k = pltpu.make_async_copy(attn_k.at[:, :, own_cols], k_all.at[me], load_sem.at[5])
    own_r = pltpu.make_async_copy(readers, rd_all.at[mine], load_sem.at[6])
    own_q.start()
    own_k.start()
    own_r.start()

    drain(st_in.at[pl.ds(0, shards - 1)], st_recv)
    rate_rows = rate_ref[my_mode, pl.ds(my_rows * 4, 4), :]
    across = jnp.exp(-float(rows) * rate_rows)

    def scan(j, carry):
        st_out[j] = carry
        return across * carry + st_in[j]

    lax.fori_loop(0, shards, scan, jnp.zeros((4, LANES), F32), unroll=4)

    @pl.loop(1, shards)
    def _(d):
        to = (me + d) % shards
        remote(st_out.at[to], start.at[me], back_send, back_recv, seq=to).start()

    start[me] = st_out[me]

    @pl.loop(1, heads)
    def _(d):
        h = (mine + d) % heads
        cols = pl.ds(pl.multiple_of(h * LANES, LANES), LANES)
        to = h * GROUP + rank
        remote(attn_k.at[:, :, cols], k_all.at[me], k_send, k_recv.at[me], seq=to).start()

    @pl.loop(1, heads)
    def _(d):
        h = (mine + d) % heads
        cols = pl.ds(pl.multiple_of(h * LANES, LANES), LANES)
        to = h * GROUP + rank
        remote(attn_q.at[:, :, cols], q_all.at[mine], q_send, q_recv, seq=to).start()
        remote(readers, rd_all.at[mine], rd_send, rd_recv, seq=to).start()

    loads[2].wait()
    loads[3].wait()
    drain(start.at[pl.ds(0, shards - 1)], back_recv)

    for half in range(halves):
        part = slice(half * 8, half * 8 + 8)
        base = half * 8 * rows
        first = []
        for m in range(modes):
            slot = (m * ltiles + half * 8) // 4
            first.append(jnp.concatenate([start[slot], start[slot + 1]], axis=0))
        skip = skip_ref[part, :]

        def filtered(t, states):
            x = xs[pl.ds(base + t, 8, stride=rows), :]
            states = tuple(decay[m, part, :] * states[m] + x for m in range(modes))
            terms = [residue_ref[m, part, :] * states[m] for m in range(modes)]
            terms.append(skip * x)
            while len(terms) > 1:
                paired = [terms[n] + terms[n + 1] for n in range(0, len(terms) - 1, 2)]
                terms = paired + terms[len(paired) * 2 :]
            ys[pl.ds(base + t, 8, stride=rows), :] = terms[0]
            return states

        lax.fori_loop(0, rows, filtered, tuple(first), unroll=4)

    def streamed(lt, acc):
        cols = pl.ds(pl.multiple_of(lt * LANES, LANES), LANES)
        convolved = ys[pl.ds(pl.multiple_of(lt * rows, rows), rows), :].astype(BF16).astype(F32)
        value = res[:, cols].astype(F32) + hq[:, cols].astype(F32) * convolved
        stream[lt] = value
        return acc + value * value

    acc = lax.fori_loop(0, ltiles, streamed, jnp.zeros((rows, LANES), F32))
    sq[plane] = lax.dot_general(
        jnp.ones((8, LANES), F32),
        acc,
        (((1,), (1,)), ((), ())),
        precision=lax.Precision.HIGHEST,
        preferred_element_type=F32,
    )
    for d in range(1, planes):
        to = (plane + d) % planes
        remote(sq.at[plane], sq.at[plane], sq_send, sq_recv, chan=to).start()
    drain(sq.at[pl.ds(0, planes - 1)], sq_recv)
    total_sq = sq[0]
    for n in range(1, planes):
        total_sq = total_sq + sq[n]
    width = float(planes * ltiles * LANES)
    scale = lax.rsqrt(total_sq / width + 1e-6).T[:, 0:1]

    def normed(h):
        value = stream[h] * scale * gain_ref[pl.ds(h, 1), :]
        return value.astype(BF16).reshape(rows // TILE, TILE, LANES)

    @pl.loop(1, heads)
    def _(d):
        h = (mine + d) % heads
        vloc[h] = normed(h)
        to = h * GROUP + rank
        remote(vloc.at[h], v_all.at[me], v_send, v_recv.at[me], seq=to).start()

    v_all[me] = normed(mine)

    def share(everything, recv, fwd):
        def pass_on(slot, to):
            remote(everything.at[slot], everything.at[slot], fwd, recv.at[slot], seq=to).start()

        pass_on(me, core_peer)
        pass_on(me, chip_peer)

        @pl.loop(1, heads)
        def _(d):
            slot = ((mine + heads - d) % heads) * GROUP + rank
            drain(everything.at[slot], recv.at[slot])
            pass_on(slot, core_peer)
            pass_on(slot, chip_peer)

        @pl.loop(0, heads)
        def _(d):
            slot = ((mine + heads - d) % heads) * GROUP + chip_rank
            drain(everything.at[slot], recv.at[slot])
            pass_on(slot, core_peer)

        @pl.loop(0, heads)
        def _(n):
            slot = n * GROUP + core_rank
            drain(everything.at[slot], recv.at[slot])
            slot = n * GROUP + far_rank
            drain(everything.at[slot], recv.at[slot])

    own_k.wait()
    share(k_all, k_recv, kf_send)

    own_q.wait()
    own_r.wait()
    drain(q_all.at[pl.ds(0, heads - 1)], q_recv)
    drain(rd_all.at[pl.ds(0, heads - 1)], rd_recv)
    to_smem = pltpu.make_async_copy(rd_all, rd_smem, load_sem.at[7])
    to_smem.start()
    to_smem.wait()

    def pick(everything, i):
        for j in range(shards):
            tiles[j * TILE : (j + 1) * TILE, :] = everything[j, rd_smem[i, 0, shards + j]]

    remote_keys = shards * TILE
    root = 1.0 / float(LANES) ** 0.5
    across_lanes = (((1,), (1,)), ((), ()))

    @pl.loop(0, heads)
    def _(i):
        query = q_all[i].reshape(rows, LANES)
        pick(k_all, i)
        lane_tile = lax.broadcasted_iota(jnp.int32, (1, LANES), 1) // TILE
        row = lax.broadcasted_iota(jnp.int32, (rows, rows), 0)
        col = lax.broadcasted_iota(jnp.int32, (rows, rows), 1)
        own = lax.dot_general(
            query, k_all[i * GROUP + rank].reshape(rows, LANES), across_lanes, preferred_element_type=F32
        )
        own = jnp.where(row >= col, own * root, -1e30)
        far = lax.dot_general(query, tiles[...], across_lanes, preferred_element_type=F32)
        masked = []
        per = LANES // TILE
        for c in range(remote_keys // LANES):
            wanted = jnp.full((1, LANES), -1, jnp.int32)
            for n in range(per):
                wanted = jnp.where(lane_tile == n, rd_smem[i, 0, c * per + n], wanted)
            masked.append(
                jnp.where(wanted >= 0, far[:, c * LANES : (c + 1) * LANES] * root, -1e30)
            )
        peak = own
        for block in masked:
            peak = jnp.maximum(peak, block)
        peak = jnp.max(peak, axis=1, keepdims=True)
        own = jnp.exp(own - peak)
        total = own
        weights[i, :, remote_keys:] = own.astype(BF16)
        for c, block in enumerate(masked):
            block = jnp.exp(block - peak)
            total = total + block
            weights[i, :, c * LANES : (c + 1) * LANES] = block.astype(BF16)
        total = jnp.sum(total, axis=1, keepdims=True)
        totals[i] = jnp.broadcast_to(1.0 / total, (rows, LANES))

    share(v_all, v_recv, vf_send)

    def attend(i):
        pick(v_all, i)
        summed = jnp.dot(weights[i, :, 0:remote_keys], tiles[...], preferred_element_type=F32)
        summed += jnp.dot(
            weights[i, :, remote_keys:],
            v_all[i * GROUP + rank].reshape(rows, LANES),
            preferred_element_type=F32,
        )
        return (summed * totals[i]).astype(BF16)

    @pl.loop(1, heads)
    def _(d):
        i = (mine + d) % heads
        o_stage[i] = attend(i)
        remote(
            o_stage.at[i], o_recv.at[mine], o_send, o_recv_sem.at[mine], seq=i * GROUP + rank
        ).start()

    o_recv[mine] = attend(mine)

    def finish(h):
        cols = pl.ds(pl.multiple_of(h * LANES, LANES), LANES)
        out_v[:, cols] = (stream[h] + o_recv[h].astype(F32)).astype(BF16)

    finish(mine)

    @pl.loop(1, heads)
    def _(d):
        h = (mine + heads - d) % heads
        drain(o_recv.at[h], o_recv_sem.at[h])
        finish(h)

    written = pltpu.make_async_copy(out_v, out, out_sem)
    written.start()

    drain(ends.at[pl.ds(0, shards - 1)], st_send)
    drain(st_out.at[pl.ds(0, shards - 1)], back_send)
    drain(sq.at[pl.ds(0, planes - 1)], sq_send)
    drain(rd_all.at[pl.ds(0, heads - 1)], rd_send)
    drain(q_all.at[pl.ds(0, heads - 1)], q_send)
    drain(q_all.at[pl.ds(0, heads - 1)], k_send)
    drain(q_all.at[pl.ds(0, heads - 1)], v_send)
    drain(q_all.at[pl.ds(0, heads - 1)], o_send)
    drain(k_all.at[pl.ds(0, 3 * heads)], kf_send)
    drain(v_all.at[pl.ds(0, 3 * heads)], vf_send)
    written.wait()


def local(
    shards,
    planes,
    residual,
    hyena_q,
    hyena_k,
    hyena_v,
    modal_residue,
    decay_rate,
    skip_gain,
    attn_q,
    attn_k,
    norm_gain,
    readers,
):
    rows, features = residual.shape
    modes = modal_residue.shape[1]
    ltiles = features // LANES
    heads = shards // GROUP

    def modal(array):
        return array.T.reshape(modes, ltiles, LANES)

    hbm = pl.BlockSpec(memory_space=pl.ANY)
    vmem = pl.BlockSpec(memory_space=pltpu.VMEM)
    dma = pltpu.SemaphoreType.DMA
    wanted = jnp.concatenate([readers, jnp.clip(readers, 0)], axis=1)
    tiled = (rows // TILE, TILE, features)
    block = (rows // TILE, TILE, LANES)
    return pl.pallas_call(
        functools.partial(kernel, shards, planes, modes),
        out_shape=jax.ShapeDtypeStruct((rows, features), BF16),
        in_specs=[hbm, hbm, hbm, hbm, vmem, vmem, vmem, hbm, hbm, vmem, hbm],
        out_specs=hbm,
        scratch_shapes=[
            pltpu.VMEM((rows, features), BF16),
            pltpu.VMEM((rows, features), BF16),
            pltpu.VMEM((rows, features), BF16),
            pltpu.VMEM((rows, features), BF16),
            pltpu.VMEM((modes, ltiles, LANES), F32),
            pltpu.VMEM((ltiles * rows, LANES), F32),
            pltpu.VMEM((ltiles * rows, LANES), F32),
            pltpu.VMEM((shards, 4, LANES), F32),
            pltpu.VMEM((shards, 4, LANES), F32),
            pltpu.VMEM((shards, 4, LANES), F32),
            pltpu.VMEM((shards, 4, LANES), F32),
            pltpu.VMEM((ltiles, rows, LANES), F32),
            pltpu.VMEM((planes, 8, LANES), F32),
            pltpu.VMEM((heads,) + block, BF16),
            pltpu.VMEM((heads,) + block, BF16),
            pltpu.VMEM((shards,) + block, BF16),
            pltpu.VMEM((shards,) + block, BF16),
            pltpu.VMEM((heads, 1, LANES), jnp.int32),
            pltpu.SMEM((heads, 1, LANES), jnp.int32),
            pltpu.VMEM((shards * TILE, LANES), BF16),
            pltpu.VMEM((heads, rows, shards * TILE + rows), BF16),
            pltpu.VMEM((heads, rows, LANES), F32),
            pltpu.VMEM((heads, rows, LANES), BF16),
            pltpu.VMEM((heads, rows, LANES), BF16),
            pltpu.VMEM((rows, features), BF16),
            dma((8,)),
            dma,
            dma,
            dma,
            dma,
            dma,
            dma,
            dma,
            dma,
            dma,
            dma,
            dma,
            dma((shards,)),
            dma,
            dma((shards,)),
            dma,
            dma,
            dma,
            dma((heads,)),
            dma,
        ],
        compiler_params=pltpu.CompilerParams(
            collective_id=0, has_side_effects=True, vmem_limit_bytes=48 * 1024 * 1024
        ),
    )(
        residual,
        hyena_q,
        hyena_k,
        hyena_v,
        modal(modal_residue),
        modal(decay_rate),
        skip_gain.reshape(ltiles, LANES),
        attn_q.reshape(tiled),
        attn_k.reshape(tiled),
        norm_gain.reshape(ltiles, LANES),
        wanted,
    )


def solution(mesh):
    spread = P("seq", "chan")
    placed = (
        spread,
        spread,
        spread,
        spread,
        P("chan", None),
        P("chan", None),
        P("chan"),
        spread,
        spread,
        P("chan"),
        P("seq", None),
    )
    return jax.shard_map(
        functools.partial(local, mesh.shape["seq"], mesh.shape["chan"]),
        mesh=mesh,
        in_specs=placed,
        out_specs=spread,
        check_vma=False,
    )
```

```python
import functools

import jax
import jax.numpy as jnp
from jax import lax
from jax.experimental import pallas as pl
from jax.experimental.pallas import tpu as pltpu
from jax.sharding import PartitionSpec as P

MESH = pl.DeviceIdType.MESH
LANES = 128
TILE = 16
GROUP = 4
LEVEL = 8
SHARE_LAG = 5
BLOCKS_AT = (3, 1, 3, 3, 6)
F32 = jnp.float32
BF16 = jnp.bfloat16


def remote(src, dst, send, recv, **where):
    return pltpu.make_async_remote_copy(
        src_ref=src,
        dst_ref=dst,
        send_sem=send,
        recv_sem=recv,
        device_id=where,
        device_id_type=MESH,
    )


def drain(ref, sem):
    pltpu.make_async_copy(ref, ref, sem).wait()


def kernel(
    shards,
    planes,
    modes,
    residual,
    hyena_q,
    hyena_k,
    hyena_v,
    residue_hbm,
    rate_hbm,
    skip_hbm,
    attn_q,
    attn_k,
    gain_hbm,
    readers_hbm,
    out,
    residue_ref,
    rate_ref,
    skip_ref,
    gain_ref,
    readers,
    hk,
    hv,
    hq,
    res,
    by_tile,
    rates,
    residues,
    decay,
    xs,
    ys,
    ends,
    st_in,
    level,
    level_in,
    st_out,
    start,
    stream,
    sq,
    vloc,
    q_all,
    k_all,
    v_all,
    rd_mine,
    rd_all,
    rd_smem,
    tiles,
    weights,
    totals,
    o_stage,
    o_recv,
    out_v,
    load_sem,
    own_sem,
    st_send,
    st_recv,
    level_send,
    level_recv,
    back_send,
    back_recv,
    sq_send,
    sq_recv,
    rd_send,
    rd_recv,
    q_send,
    q_recv,
    k_send,
    k_recv,
    v_send,
    v_recv,
    kf_send,
    vf_send,
    o_send,
    o_recv_sem,
    out_sem,
):
    me = lax.axis_index("seq")
    plane = lax.axis_index("chan")
    heads = shards // GROUP
    mine = me // GROUP
    core = me % 2
    side = (me // 2) % 2
    core_peer = me + 1 - 2 * core
    chip_peer = me + 2 - 4 * side
    middle = shards // 2
    half = me // middle
    turned = (mine // 2) % 2
    my_half = (side + turned) % 2
    my_row = (me % middle) // 2
    place = me % LEVEL
    level_at = me // LEVEL
    levels = shards // LEVEL
    rows = hk.shape[0]
    ltiles = hk.shape[1] // LANES

    loads = [
        pltpu.make_async_copy(src, dst, load_sem.at[n])
        for n, (src, dst) in enumerate(
            (
                (hyena_k, hk),
                (hyena_v, hv),
                (rate_hbm, rate_ref),
                (residue_hbm, residue_ref),
                (readers_hbm, readers),
                (skip_hbm, skip_ref),
                (gain_hbm, gain_ref),
                (hyena_q, hq),
                (residual, res),
            )
        )
    ]
    for load in loads:
        load.start()

    barrier = pltpu.get_barrier_semaphore()

    @pl.loop(0, LEVEL // 2)
    def _(n):
        to = level_at * LEVEL + 2 * n + 1 - core
        pl.semaphore_signal(barrier, inc=1, device_id={"seq": to}, device_id_type=MESH)

    for d in range(1, planes):
        to = (plane + d) % planes
        pl.semaphore_signal(barrier, inc=1, device_id={"chan": to}, device_id_type=MESH)

    @pl.loop(1, middle)
    def _(d):
        to = (me + 2 * d) % shards
        pl.semaphore_signal(barrier, inc=1, device_id={"seq": to}, device_id_type=MESH)

    def order(n):
        return heads // 2 + (1 - n % 2) * (n // 2) - (n % 2) * ((n + 1) // 2)

    def columns(h):
        return pl.ds(pl.multiple_of(h * LANES, LANES), LANES)

    def reader_of(h):
        return h * GROUP + 2 * ((half + h // 2) % 2) + core

    def holder_of(h):
        return h * GROUP + 2 * (half * ((1 + h // 2) % 2) + (1 - half) * side) + core

    at_home = half == my_half
    held_here = jnp.logical_or(half == 0, at_home)

    def send_keys(low, high):
        @pl.loop(low, high)
        def _(n):
            send_key(n)

    def send_key(n):
        h = (mine + order(n)) % heads
        remote(
            attn_k.at[:, :, columns(h)], k_all.at[me], k_send, k_recv.at[me], seq=holder_of(h)
        ).start()

    def send_query(n):
        h = (mine + order(n)) % heads
        to = reader_of(h)
        remote(rd_mine, rd_all.at[my_row], rd_send, rd_recv.at[my_row], seq=to).start()
        remote(
            attn_q.at[:, :, columns(h)], q_all.at[my_row], q_send, q_recv.at[my_row], seq=to
        ).start()

    def send_queries(low, high):
        @pl.loop(low, high)
        def _(n):
            send_query(n)

    def send_blocks(low, high):
        split = heads - 1
        if low < min(high, split):
            send_keys(low, min(high, split))
        if max(low, split) < high:
            send_queries(max(low, split) - split, high - split)

    def keep_key():
        @pl.when(held_here)
        def _():
            pltpu.make_async_copy(
                attn_k.at[:, :, columns(mine)], k_all.at[me], k_recv.at[me]
            ).start()

        @pl.when(jnp.logical_not(held_here))
        def _():
            remote(
                attn_k.at[:, :, columns(mine)],
                k_all.at[me],
                own_sem.at[0],
                k_recv.at[me],
                seq=chip_peer,
            ).start()

    def keep_query():
        @pl.when(at_home)
        def _():
            pltpu.make_async_copy(
                attn_q.at[:, :, columns(mine)], q_all.at[my_row], q_recv.at[my_row]
            ).start()
            pltpu.make_async_copy(rd_mine, rd_all.at[my_row], rd_recv.at[my_row]).start()

        @pl.when(jnp.logical_not(at_home))
        def _():
            remote(
                attn_q.at[:, :, columns(mine)],
                q_all.at[my_row],
                own_sem.at[1],
                q_recv.at[my_row],
                seq=chip_peer,
            ).start()
            remote(
                rd_mine, rd_all.at[my_row], own_sem.at[2], rd_recv.at[my_row], seq=chip_peer
            ).start()

    pl.semaphore_wait(barrier, LEVEL // 2 + planes - 1 + middle - 1)
    at_entry, at_stretch, at_share, at_level, at_back = BLOCKS_AT
    send_blocks(0, at_entry)
    issued = at_entry

    loads[2].wait()
    loads[3].wait()
    loads[4].wait()

    def spread_modes(lt, _):
        cols = pl.ds(pl.multiple_of(lt * LANES, LANES), LANES)
        at = pl.ds(pl.multiple_of(lt * modes, modes), modes)
        by_tile[0, at, :] = rate_ref[:, cols]
        by_tile[1, at, :] = residue_ref[:, cols]
        return _

    lax.fori_loop(0, ltiles, spread_modes, 0)
    for m in range(modes):
        for part in range(ltiles // 8):
            of_mode = pl.ds(part * 8 * modes + m, 8, stride=modes)
            sub = slice(m * ltiles + part * 8, m * ltiles + part * 8 + 8)
            rate = by_tile[0, of_mode, :]
            rates[sub, :] = rate
            decay[sub, :] = jnp.exp(-rate)
            residues[sub, :] = by_tile[1, of_mode, :]
    wanted = readers[...]
    rd_mine[...] = jnp.zeros_like(rd_mine)
    rd_mine[0:1, 0:shards] = wanted
    rd_mine[1:2, 0:shards] = jnp.maximum(wanted, 0)
    loads[0].wait()
    loads[1].wait()

    @pl.loop(0, ltiles)
    def _(lt):
        cols = pl.ds(pl.multiple_of(lt * LANES, LANES), LANES)
        product = (hk[:, cols].astype(F32) * hv[:, cols].astype(F32)).astype(BF16)
        xs[pl.ds(pl.multiple_of(lt * rows, rows), rows), :] = product.astype(F32)

    per_place = modes // LEVEL
    parts = ltiles // 8

    def mode_rows(m, part):
        return slice(m * ltiles + part * 8, m * ltiles + part * 8 + 8)

    def share_rows(m, part):
        at = (m % per_place) * ltiles + part * 8
        return slice(at, at + 8)

    for part in range(parts):
        base = part * 8 * rows

        def advance(t, states):
            x = xs[pl.ds(base + t, 8, stride=rows), :]
            return tuple(decay[mode_rows(m, part), :] * states[m] + x for m in range(modes))

        def stretch(n, states, part=part, advance=advance):
            if at_stretch:
                send_key(at_entry + part * 2 + n)
            span = rows // 2

            def inner(t, states):
                return advance(n * span + t, states)

            return lax.fori_loop(0, span, inner, states, unroll=4)

        states = lax.fori_loop(
            0, 2, stretch, tuple(jnp.zeros((8, LANES), F32) for _ in range(modes))
        )
        for m in range(modes):
            ends[m // per_place, share_rows(m, part), :] = states[m]

    issued += 2 * parts * at_stretch

    @pl.loop(1, LEVEL)
    def _(d):
        at = (place + d) % LEVEL
        to = level_at * LEVEL + at
        remote(ends.at[at], st_in.at[place], st_send, st_recv, seq=to).start()

    st_in[place] = ends[place]
    send_blocks(issued, issued + at_share)
    issued += at_share

    my_rates = rates[pl.ds(pl.multiple_of(place * per_place * ltiles, 8), per_place * ltiles), :]
    across = jnp.exp(-float(rows) * my_rates)
    across_level = jnp.exp(-float(rows * LEVEL) * my_rates)
    drain(st_in.at[pl.ds(0, LEVEL - 1)], st_recv)
    carry = st_in[0]
    for n in range(1, LEVEL):
        carry = across * carry + st_in[n]
    level[...] = carry

    @pl.loop(level_at + 1, levels)
    def _(to):
        remote(
            level,
            level_in.at[level_at],
            level_send.at[to],
            level_recv.at[level_at],
            seq=to * LEVEL + place,
        ).start()

    send_blocks(issued, issued + at_level)
    issued += at_level

    def before(n, carry):
        drain(level_in.at[n], level_recv.at[n])
        return across_level * carry + level_in[n]

    carry = lax.fori_loop(0, level_at, before, jnp.zeros_like(carry))
    for n in range(LEVEL):
        st_out[n] = carry
        carry = across * carry + st_in[n]

    @pl.loop(1, LEVEL)
    def _(d):
        at = (place + d) % LEVEL
        to = level_at * LEVEL + at
        remote(st_out.at[at], start.at[place], back_send, back_recv, seq=to).start()

    start[place] = st_out[place]
    send_blocks(issued, issued + at_back)
    issued += at_back
    keep_key()
    loads[5].wait()
    loads[6].wait()
    loads[7].wait()
    loads[8].wait()
    drain(start.at[pl.ds(0, LEVEL - 1)], back_recv)

    for part in range(parts):
        base = part * 8 * rows
        skip = skip_ref[part * 8 : part * 8 + 8, :]

        def filtered(t, states):
            x = xs[pl.ds(base + t, 8, stride=rows), :]
            states = tuple(decay[mode_rows(m, part), :] * states[m] + x for m in range(modes))
            terms = [residues[mode_rows(m, part), :] * states[m] for m in range(modes)]
            terms.append(skip * x)
            while len(terms) > 1:
                paired = [terms[n] + terms[n + 1] for n in range(0, len(terms) - 1, 2)]
                terms = paired + terms[len(paired) * 2 :]
            ys[pl.ds(base + t, 8, stride=rows), :] = terms[0]
            return states

        first = tuple(start[m // per_place, share_rows(m, part), :] for m in range(modes))

        lax.fori_loop(0, rows, filtered, first, unroll=4)

    def streamed(lt, acc):
        cols = columns(lt)
        convolved = ys[pl.ds(pl.multiple_of(lt * rows, rows), rows), :].astype(BF16).astype(F32)
        value = res[:, cols].astype(F32) + hq[:, cols].astype(F32) * convolved
        stream[lt] = value
        return acc + value * value

    acc = lax.fori_loop(0, ltiles, streamed, jnp.zeros((rows, LANES), F32))
    sq[plane] = lax.dot_general(
        jnp.ones((8, LANES), F32),
        acc,
        (((1,), (1,)), ((), ())),
        precision=lax.Precision.HIGHEST,
        preferred_element_type=F32,
    )
    for d in range(1, planes):
        to = (plane + d) % planes
        remote(sq.at[plane], sq.at[plane], sq_send, sq_recv, chan=to).start()
    send_blocks(issued, 2 * (heads - 1))
    keep_query()

    early = heads // 2

    def sharing(everything, recv, fwd):
        def pass_on(slot, to):
            remote(everything.at[slot], everything.at[slot], fwd, recv.at[slot], seq=to).start()

        def share_slot(slot, to_chip):
            drain(everything.at[slot], recv.at[slot])
            if to_chip:
                pass_on(slot, chip_peer)
            pass_on(slot, core_peer)

        def share_far(n):
            slot = n * GROUP + 2 * (1 - side) + core
            share_slot(slot, False)

        def share_from(n):
            group = (mine + heads - order(n)) % heads

            @pl.when(group < early)
            def _():
                share_slot(group * GROUP + 2 * side + core, True)

            @pl.when(jnp.logical_and(group >= early, my_half == 1))
            def _():
                share_slot(group * GROUP + core, False)
                share_slot(group * GROUP + 2 + core, False)

        def arrive():
            @pl.loop(0, middle // 2)
            def _(n):
                slot = 2 * n + 1 - core
                drain(everything.at[slot], recv.at[slot])

            @pl.when(my_half == 1)
            def _():
                @pl.loop(middle // 2, middle)
                def _(n):
                    slot = 2 * n + 1 - core
                    drain(everything.at[slot], recv.at[slot])

        return share_from, share_far, arrive

    key_from, far_key, keys_arrive = sharing(k_all, k_recv, kf_send)
    pl.loop(0, heads)(key_from)

    def far_keys():
        pl.loop(0, early)(far_key)

    drain(sq.at[pl.ds(0, planes - 1)], sq_recv)
    total_sq = sq[0]
    for n in range(1, planes):
        total_sq = total_sq + sq[n]
    width = float(planes * ltiles * LANES)
    scale = lax.rsqrt(total_sq / width + 1e-6).T[:, 0:1]

    def normed(h):
        value = stream[h] * scale * gain_ref[pl.ds(h, 1), :]
        return value.astype(BF16).reshape(rows // TILE, TILE, LANES)

    @pl.loop(0, heads - 1)
    def _(n):
        h = (mine + order(n)) % heads
        vloc[h] = normed(h)
        remote(vloc.at[h], v_all.at[me], v_send, v_recv.at[me], seq=holder_of(h)).start()

    vloc[mine] = normed(mine)

    @pl.when(held_here)
    def _():
        pltpu.make_async_copy(vloc.at[mine], v_all.at[me], v_recv.at[me]).start()

    @pl.when(jnp.logical_not(held_here))
    def _():
        remote(
            vloc.at[mine], v_all.at[me], own_sem.at[3], v_recv.at[me], seq=chip_peer
        ).start()

    far_keys()
    keys_arrive()

    @pl.loop(0, heads)
    def _(n):
        drain(rd_all.at[n], rd_recv.at[n])

    to_smem = pltpu.make_async_copy(rd_all, rd_smem, load_sem.at[9])
    to_smem.start()
    to_smem.wait()

    def pick(everything, i, count):
        for j in range(count):
            tiles[j * TILE : (j + 1) * TILE, :] = everything[j, rd_smem[i, 1, j]]

    root = 1.4426950408889634 / float(LANES) ** 0.5
    lanes = (((1,), (1,)), ((), ()))

    def weigh(i, count):
        keys = count * TILE
        query = q_all[i].reshape(rows, LANES)
        shard = my_half * middle + 2 * i + core
        pick(k_all, i, count)
        lane_tile = lax.broadcasted_iota(jnp.int32, (1, LANES), 1) // TILE
        row = lax.broadcasted_iota(jnp.int32, (rows, rows), 0)
        col = lax.broadcasted_iota(jnp.int32, (rows, rows), 1)
        own = lax.dot_general(
            query, k_all[shard].reshape(rows, LANES), lanes, preferred_element_type=F32
        )
        far = lax.dot_general(query, tiles[0:keys, :], lanes, preferred_element_type=F32)
        blocks = [jnp.where(row >= col, own * root, -1e30)]
        zero = jnp.zeros((1, LANES), F32)
        per = LANES // TILE
        for c in range(keys // LANES):
            wanted = jnp.full((1, LANES), -1, jnp.int32)
            for n in range(per):
                wanted = jnp.where(lane_tile == n, rd_smem[i, 0, c * per + n], wanted)
            block = far[:, c * LANES : (c + 1) * LANES] * root
            blocks.append(block + jnp.where(wanted >= 0, zero, -1e30))
        peak = blocks[0]
        for block in blocks[1:]:
            peak = jnp.maximum(peak, block)
        peak = jnp.max(peak, axis=1, keepdims=True)
        total = jnp.zeros((rows, LANES), F32)
        for c, block in enumerate(blocks):
            block = jnp.exp2(block - peak)
            total = total + block
            weights[i, :, c * LANES : (c + 1) * LANES] = block.astype(BF16)
        total = jnp.sum(total, axis=1, keepdims=True)
        totals[i] = jnp.broadcast_to(1.0 / total, (rows, LANES))

    share_from, share_far, arrive = sharing(v_all, v_recv, vf_send)

    @pl.loop(0, heads)
    def _(n):
        drain(q_all.at[n], q_recv.at[n])

        @pl.when(n >= SHARE_LAG)
        def _():
            share_from(n - SHARE_LAG)

        @pl.when(my_half == 0)
        def _():
            weigh(n, middle)

        @pl.when(my_half == 1)
        def _():
            weigh(n, shards)

    @pl.loop(heads - SHARE_LAG, heads)
    def _(n):
        share_from(n)

    pl.loop(0, early)(share_far)
    arrive()

    def attend(i, count):
        keys = count * TILE
        pick(v_all, i, count)
        shard = my_half * middle + 2 * i + core
        summed = jnp.dot(
            weights[i, :, LANES : LANES + keys], tiles[0:keys, :], preferred_element_type=F32
        )
        summed += jnp.dot(
            weights[i, :, 0:LANES],
            v_all[shard].reshape(rows, LANES),
            preferred_element_type=F32,
        )
        o_stage[i] = (summed * totals[i]).astype(BF16)

    @pl.loop(0, heads)
    def _(n):
        i = (mine + 5 * n) % heads
        shard = my_half * middle + 2 * i + core

        @pl.when(my_half == 0)
        def _():
            attend(i, middle)

        @pl.when(my_half == 1)
        def _():
            attend(i, shards)

        @pl.when(shard != me)
        def _():
            remote(
                o_stage.at[i], o_recv.at[mine], o_send.at[i], o_recv_sem.at[mine], seq=shard
            ).start()

        @pl.when(shard == me)
        def _():
            pltpu.make_async_copy(o_stage.at[i], o_recv.at[mine], o_recv_sem.at[mine]).start()

    @pl.loop(0, heads)
    def _(n):
        h = (my_row + heads - n) % heads
        drain(o_recv.at[h], o_recv_sem.at[h])
        cols = columns(h)
        out_v[:, cols] = (stream[h] + o_recv[h].astype(F32)).astype(BF16)

    written = pltpu.make_async_copy(out_v, out, out_sem)
    written.start()

    drain(ends.at[pl.ds(0, LEVEL - 1)], st_send)
    drain(st_out.at[pl.ds(0, LEVEL - 1)], back_send)
    drain(sq.at[pl.ds(0, planes - 1)], sq_send)
    drain(rd_all.at[pl.ds(0, heads - 1)], rd_send)
    drain(q_all.at[pl.ds(0, heads - 1)], q_send)
    drain(q_all.at[pl.ds(0, heads - 1)], k_send)
    drain(q_all.at[pl.ds(0, heads - 1)], v_send)

    @pl.loop(level_at + 1, levels)
    def _(to):
        drain(level, level_send.at[to])

    @pl.when(jnp.logical_not(held_here))
    def _():
        drain(q_all.at[0], own_sem.at[0])
        drain(q_all.at[0], own_sem.at[3])

    @pl.when(jnp.logical_not(at_home))
    def _():
        drain(q_all.at[0], own_sem.at[1])
        drain(rd_all.at[0], own_sem.at[2])

    for fwd in (kf_send, vf_send):

        @pl.when(my_half == 0)
        def _():
            drain(k_all.at[pl.ds(0, 3 * early)], fwd)

        @pl.when(my_half == 1)
        def _():
            drain(k_all.at[pl.ds(0, 5 * early)], fwd)

    @pl.loop(0, heads)
    def _(i):
        @pl.when(my_half * middle + 2 * i + core != me)
        def _():
            drain(o_stage.at[i], o_send.at[i])

    written.wait()


def local(
    shards,
    planes,
    residual,
    hyena_q,
    hyena_k,
    hyena_v,
    modal_residue,
    decay_rate,
    skip_gain,
    attn_q,
    attn_k,
    norm_gain,
    readers,
):
    rows, features = residual.shape
    modes = modal_residue.shape[1]
    ltiles = features // LANES
    heads = shards // GROUP

    hbm = pl.BlockSpec(memory_space=pl.ANY)
    dma = pltpu.SemaphoreType.DMA
    tiled = (rows // TILE, TILE, features)
    block = (rows // TILE, TILE, LANES)
    share = (modes * ltiles // LEVEL, LANES)
    return pl.pallas_call(
        functools.partial(kernel, shards, planes, modes),
        out_shape=jax.ShapeDtypeStruct((rows, features), BF16),
        in_specs=[hbm] * 11,
        out_specs=hbm,
        scratch_shapes=[
            pltpu.VMEM((modes, features), F32),
            pltpu.VMEM((modes, features), F32),
            pltpu.VMEM((ltiles, LANES), F32),
            pltpu.VMEM((ltiles, LANES), F32),
            pltpu.VMEM((1, shards), jnp.int32),
            pltpu.VMEM((rows, features), BF16),
            pltpu.VMEM((rows, features), BF16),
            pltpu.VMEM((rows, features), BF16),
            pltpu.VMEM((rows, features), BF16),
            pltpu.VMEM((2, ltiles * modes, LANES), F32),
            pltpu.VMEM((modes * ltiles, LANES), F32),
            pltpu.VMEM((modes * ltiles, LANES), F32),
            pltpu.VMEM((modes * ltiles, LANES), F32),
            pltpu.VMEM((ltiles * rows, LANES), F32),
            pltpu.VMEM((ltiles * rows, LANES), F32),
            pltpu.VMEM((LEVEL,) + share, F32),
            pltpu.VMEM((LEVEL,) + share, F32),
            pltpu.VMEM(share, F32),
            pltpu.VMEM((shards // LEVEL,) + share, F32),
            pltpu.VMEM((LEVEL,) + share, F32),
            pltpu.VMEM((LEVEL,) + share, F32),
            pltpu.VMEM((ltiles, rows, LANES), F32),
            pltpu.VMEM((planes, 8, LANES), F32),
            pltpu.VMEM((heads,) + block, BF16),
            pltpu.VMEM((heads,) + block, BF16),
            pltpu.VMEM((shards,) + block, BF16),
            pltpu.VMEM((shards,) + block, BF16),
            pltpu.VMEM((2, LANES), jnp.int32),
            pltpu.VMEM((heads, 2, LANES), jnp.int32),
            pltpu.SMEM((heads, 2, LANES), jnp.int32),
            pltpu.VMEM((shards * TILE, LANES), BF16),
            pltpu.VMEM((heads, rows, shards * TILE + rows), BF16),
            pltpu.VMEM((heads, rows, LANES), F32),
            pltpu.VMEM((heads, rows, LANES), BF16),
            pltpu.VMEM((heads, rows, LANES), BF16),
            pltpu.VMEM((rows, features), BF16),
            dma((10,)),
            dma((4,)),
            dma,
            dma,
            dma((shards // LEVEL,)),
            dma((shards // LEVEL,)),
            dma,
            dma,
            dma,
            dma,
            dma,
            dma((heads,)),
            dma,
            dma((heads,)),
            dma,
            dma((shards,)),
            dma,
            dma((shards,)),
            dma,
            dma,
            dma((heads,)),
            dma((heads,)),
            dma,
        ],
        compiler_params=pltpu.CompilerParams(
            collective_id=0, has_side_effects=True, vmem_limit_bytes=60 * 1024 * 1024
        ),
    )(
        residual,
        hyena_q,
        hyena_k,
        hyena_v,
        modal_residue.T,
        decay_rate.T,
        skip_gain.reshape(ltiles, LANES),
        attn_q.reshape(tiled),
        attn_k.reshape(tiled),
        norm_gain.reshape(ltiles, LANES),
        readers,
    )


def solution(mesh):
    spread = P("seq", "chan")
    placed = (
        spread,
        spread,
        spread,
        spread,
        P("chan", None),
        P("chan", None),
        P("chan"),
        spread,
        spread,
        P("chan"),
        P("seq", None),
    )
    return jax.shard_map(
        functools.partial(local, mesh.shape["seq"], mesh.shape["chan"]),
        mesh=mesh,
        in_specs=placed,
        out_specs=spread,
        check_vma=False,
    )
```

```python
import functools

import jax
import jax.numpy as jnp
from jax import lax
from jax.experimental import pallas as pl
from jax.experimental.pallas import tpu as pltpu
from jax.sharding import PartitionSpec as P

MESH = pl.DeviceIdType.MESH
LANES = 128
TILE = 16
GROUP = 4
LEVEL = 8
SHARE_LAG = 4
VALUES_AHEAD = 15
BLOCKS_AT = (4, 1, 4, 6, 6)
F32 = jnp.float32
BF16 = jnp.bfloat16


def remote(src, dst, send, recv, **where):
    return pltpu.make_async_remote_copy(
        src_ref=src,
        dst_ref=dst,
        send_sem=send,
        recv_sem=recv,
        device_id=where,
        device_id_type=MESH,
    )


def drain(ref, sem):
    pltpu.make_async_copy(ref, ref, sem).wait()


def kernel(
    shards,
    planes,
    modes,
    residual,
    hyena_q,
    hyena_k,
    hyena_v,
    residue_hbm,
    rate_hbm,
    skip_hbm,
    attn_q,
    attn_k,
    gain_hbm,
    readers_hbm,
    out,
    residue_ref,
    rate_ref,
    skip_ref,
    gain_ref,
    readers,
    hk,
    hv,
    hq,
    res,
    by_tile,
    rates,
    residues,
    decay,
    xs,
    ys,
    ends,
    st_in,
    level,
    level_in,
    st_out,
    start,
    stream,
    sq,
    vloc,
    q_all,
    k_all,
    v_all,
    rd_mine,
    rd_all,
    rd_smem,
    tiles,
    weights,
    totals,
    o_stage,
    o_recv,
    out_v,
    load_sem,
    own_sem,
    st_send,
    st_recv,
    level_send,
    level_recv,
    back_send,
    back_recv,
    sq_send,
    sq_recv,
    rd_send,
    rd_recv,
    q_send,
    q_recv,
    k_send,
    k_recv,
    v_send,
    v_recv,
    kf_send,
    vf_send,
    o_send,
    o_recv_sem,
    out_sem,
):
    me = lax.axis_index("seq")
    plane = lax.axis_index("chan")
    heads = shards // GROUP
    mine = me // GROUP
    core = me % 2
    side = (me // 2) % 2
    core_peer = me + 1 - 2 * core
    chip_peer = me + 2 - 4 * side
    middle = shards // 2
    half = me // middle
    turned = (mine // 2) % 2
    my_half = (side + turned) % 2
    my_row = (me % middle) // 2
    place = me % LEVEL
    level_at = me // LEVEL
    levels = shards // LEVEL
    rows = hk.shape[0]
    ltiles = hk.shape[1] // LANES

    loads = [
        pltpu.make_async_copy(src, dst, load_sem.at[n])
        for n, (src, dst) in enumerate(
            (
                (hyena_k, hk),
                (hyena_v, hv),
                (rate_hbm, rate_ref),
                (residue_hbm, residue_ref),
                (readers_hbm, readers),
                (skip_hbm, skip_ref),
                (gain_hbm, gain_ref),
                (hyena_q, hq),
                (residual, res),
            )
        )
    ]
    for load in loads:
        load.start()

    barrier = pltpu.get_barrier_semaphore()

    @pl.loop(0, LEVEL // 2)
    def _(n):
        to = level_at * LEVEL + 2 * n + 1 - core
        pl.semaphore_signal(barrier, inc=1, device_id={"seq": to}, device_id_type=MESH)

    for d in range(1, planes):
        to = (plane + d) % planes
        pl.semaphore_signal(barrier, inc=1, device_id={"chan": to}, device_id_type=MESH)

    @pl.loop(1, middle)
    def _(d):
        to = (me + 2 * d) % shards
        pl.semaphore_signal(barrier, inc=1, device_id={"seq": to}, device_id_type=MESH)

    def order(n):
        return heads // 2 + (1 - n % 2) * (n // 2) - (n % 2) * ((n + 1) // 2)

    def columns(h):
        return pl.ds(pl.multiple_of(h * LANES, LANES), LANES)

    def reader_of(h):
        return h * GROUP + 2 * ((half + h // 2) % 2) + core

    def holder_of(h):
        return h * GROUP + 2 * (half * ((1 + h // 2) % 2) + (1 - half) * side) + core

    at_home = half == my_half
    held_here = jnp.logical_or(half == 0, at_home)

    def send_keys(low, high):
        @pl.loop(low, high)
        def _(n):
            send_key(n)

    def send_key(n):
        h = (mine + order(n)) % heads
        remote(
            attn_k.at[:, :, columns(h)], k_all.at[me], k_send, k_recv.at[me], seq=holder_of(h)
        ).start()

    def send_query(n):
        h = (mine + order(n)) % heads
        to = reader_of(h)
        remote(rd_mine, rd_all.at[my_row], rd_send, rd_recv.at[my_row], seq=to).start()
        remote(
            attn_q.at[:, :, columns(h)], q_all.at[my_row], q_send, q_recv.at[my_row], seq=to
        ).start()

    def send_queries(low, high):
        @pl.loop(low, high)
        def _(n):
            send_query(n)

    def send_blocks(low, high):
        split = heads - 1
        if low < min(high, split):
            send_keys(low, min(high, split))
        if max(low, split) < high:
            send_queries(max(low, split) - split, high - split)

    def keep_key():
        @pl.when(held_here)
        def _():
            pltpu.make_async_copy(
                attn_k.at[:, :, columns(mine)], k_all.at[me], k_recv.at[me]
            ).start()

        @pl.when(jnp.logical_not(held_here))
        def _():
            remote(
                attn_k.at[:, :, columns(mine)],
                k_all.at[me],
                own_sem.at[0],
                k_recv.at[me],
                seq=chip_peer,
            ).start()

    def keep_query():
        @pl.when(at_home)
        def _():
            pltpu.make_async_copy(
                attn_q.at[:, :, columns(mine)], q_all.at[my_row], q_recv.at[my_row]
            ).start()
            pltpu.make_async_copy(rd_mine, rd_all.at[my_row], rd_recv.at[my_row]).start()

        @pl.when(jnp.logical_not(at_home))
        def _():
            remote(
                attn_q.at[:, :, columns(mine)],
                q_all.at[my_row],
                own_sem.at[1],
                q_recv.at[my_row],
                seq=chip_peer,
            ).start()
            remote(
                rd_mine, rd_all.at[my_row], own_sem.at[2], rd_recv.at[my_row], seq=chip_peer
            ).start()

    pl.semaphore_wait(barrier, LEVEL // 2 + planes - 1 + middle - 1)
    at_entry, at_stretch, at_share, at_level, at_back = BLOCKS_AT
    keep_key()
    send_blocks(0, at_entry)
    issued = at_entry

    loads[2].wait()
    loads[3].wait()
    loads[4].wait()

    def spread_modes(lt, _):
        cols = pl.ds(pl.multiple_of(lt * LANES, LANES), LANES)
        at = pl.ds(pl.multiple_of(lt * modes, modes), modes)
        by_tile[0, at, :] = rate_ref[:, cols]
        by_tile[1, at, :] = residue_ref[:, cols]
        return _

    lax.fori_loop(0, ltiles, spread_modes, 0)
    for m in range(modes):
        for part in range(ltiles // 8):
            of_mode = pl.ds(part * 8 * modes + m, 8, stride=modes)
            sub = slice(m * ltiles + part * 8, m * ltiles + part * 8 + 8)
            rate = by_tile[0, of_mode, :]
            rates[sub, :] = rate
            decay[sub, :] = jnp.exp(-rate)
            residues[sub, :] = by_tile[1, of_mode, :]
    wanted = readers[...]
    rd_mine[...] = jnp.zeros_like(rd_mine)
    rd_mine[0:1, 0:shards] = wanted
    rd_mine[1:2, 0:shards] = jnp.maximum(wanted, 0)
    loads[0].wait()
    loads[1].wait()

    @pl.loop(0, ltiles)
    def _(lt):
        cols = pl.ds(pl.multiple_of(lt * LANES, LANES), LANES)
        product = (hk[:, cols].astype(F32) * hv[:, cols].astype(F32)).astype(BF16)
        xs[pl.ds(pl.multiple_of(lt * rows, rows), rows), :] = product.astype(F32)

    per_place = modes // LEVEL
    parts = ltiles // 8

    def mode_rows(m, part):
        return slice(m * ltiles + part * 8, m * ltiles + part * 8 + 8)

    def share_rows(m, part):
        at = (m % per_place) * ltiles + part * 8
        return slice(at, at + 8)

    for part in range(parts):
        base = part * 8 * rows

        def advance(t, states):
            x = xs[pl.ds(base + t, 8, stride=rows), :]
            return tuple(decay[mode_rows(m, part), :] * states[m] + x for m in range(modes))

        def stretch(n, states, part=part, advance=advance):
            if at_stretch:
                send_key(at_entry + part * 2 + n)
            span = rows // 2

            def inner(t, states):
                return advance(n * span + t, states)

            return lax.fori_loop(0, span, inner, states, unroll=4)

        states = lax.fori_loop(
            0, 2, stretch, tuple(jnp.zeros((8, LANES), F32) for _ in range(modes))
        )
        for m in range(modes):
            ends[m // per_place, share_rows(m, part), :] = states[m]

    issued += 2 * parts * at_stretch

    @pl.loop(1, LEVEL)
    def _(d):
        at = (place + d) % LEVEL
        to = level_at * LEVEL + at
        remote(ends.at[at], st_in.at[place], st_send, st_recv, seq=to).start()

    st_in[place] = ends[place]
    send_blocks(issued, issued + at_share)
    issued += at_share

    my_rates = rates[pl.ds(pl.multiple_of(place * per_place * ltiles, 8), per_place * ltiles), :]
    across = jnp.exp(-float(rows) * my_rates)
    across_level = jnp.exp(-float(rows * LEVEL) * my_rates)
    drain(st_in.at[pl.ds(0, LEVEL - 1)], st_recv)
    carry = st_in[0]
    for n in range(1, LEVEL):
        carry = across * carry + st_in[n]
    level[...] = carry

    @pl.loop(level_at + 1, levels)
    def _(to):
        remote(
            level,
            level_in.at[level_at],
            level_send.at[to],
            level_recv.at[level_at],
            seq=to * LEVEL + place,
        ).start()

    send_blocks(issued, issued + at_level)
    issued += at_level

    def before(n, carry):
        drain(level_in.at[n], level_recv.at[n])
        return across_level * carry + level_in[n]

    carry = lax.fori_loop(0, level_at, before, jnp.zeros_like(carry))
    for n in range(LEVEL):
        st_out[n] = carry
        carry = across * carry + st_in[n]

    @pl.loop(1, LEVEL)
    def _(d):
        at = (place + d) % LEVEL
        to = level_at * LEVEL + at
        remote(st_out.at[at], start.at[place], back_send, back_recv, seq=to).start()

    start[place] = st_out[place]
    send_blocks(issued, issued + at_back)
    issued += at_back
    loads[5].wait()
    loads[6].wait()
    loads[7].wait()
    loads[8].wait()
    drain(start.at[pl.ds(0, LEVEL - 1)], back_recv)

    early = heads // 2

    def sharing(everything, recv, fwd):
        def pass_on(slot, to):
            remote(everything.at[slot], everything.at[slot], fwd, recv.at[slot], seq=to).start()

        def share_slot(slot, to_chip):
            drain(everything.at[slot], recv.at[slot])
            if to_chip:
                pass_on(slot, chip_peer)
            pass_on(slot, core_peer)

        def share_far(n):
            slot = n * GROUP + 2 * (1 - side) + core
            share_slot(slot, False)

        def share_from(n):
            group = (mine + heads - order(n)) % heads

            @pl.when(group < early)
            def _():
                share_slot(group * GROUP + 2 * side + core, True)

            @pl.when(jnp.logical_and(group >= early, my_half == 1))
            def _():
                share_slot(group * GROUP + core, False)
                share_slot(group * GROUP + 2 + core, False)

        def share_step(k):
            near = (k + mine) % early

            @pl.when(k < early)
            def _():
                share_slot(near * GROUP + 2 * side + core, True)

            @pl.when(jnp.logical_and(k >= early, k < 2 * early))
            def _():
                share_far(near)

            @pl.when(jnp.logical_and(k >= 2 * early, my_half == 1))
            def _():
                share_slot((early + near) * GROUP + core, False)
                share_slot((early + near) * GROUP + 2 + core, False)

        def arrive():
            @pl.loop(0, middle // 2)
            def _(n):
                slot = 2 * n + 1 - core
                drain(everything.at[slot], recv.at[slot])

            @pl.when(my_half == 1)
            def _():
                @pl.loop(middle // 2, middle)
                def _(n):
                    slot = 2 * n + 1 - core
                    drain(everything.at[slot], recv.at[slot])

        return share_from, share_step, share_far, arrive

    key_from, _, far_key, keys_arrive = sharing(k_all, k_recv, kf_send)
    for part in range(parts):
        base = part * 8 * rows
        skip = skip_ref[part * 8 : part * 8 + 8, :]

        def filtered(t, states):
            x = xs[pl.ds(base + t, 8, stride=rows), :]
            states = tuple(decay[mode_rows(m, part), :] * states[m] + x for m in range(modes))
            terms = [residues[mode_rows(m, part), :] * states[m] for m in range(modes)]
            terms.append(skip * x)
            while len(terms) > 1:
                paired = [terms[n] + terms[n + 1] for n in range(0, len(terms) - 1, 2)]
                terms = paired + terms[len(paired) * 2 :]
            ys[pl.ds(base + t, 8, stride=rows), :] = terms[0]
            return states

        first = tuple(start[m // per_place, share_rows(m, part), :] for m in range(modes))

        lax.fori_loop(0, rows, filtered, first, unroll=4)
        steps = heads // parts
        pl.loop(part * steps, (part + 1) * steps)(key_from)
        left = 2 * (heads - 1) - issued
        send_blocks(issued + left * part // parts, issued + left * (part + 1) // parts)

    def streamed(lt, acc):
        cols = columns(lt)
        convolved = ys[pl.ds(pl.multiple_of(lt * rows, rows), rows), :].astype(BF16).astype(F32)
        value = res[:, cols].astype(F32) + hq[:, cols].astype(F32) * convolved
        stream[lt] = value
        return acc + value * value

    acc = lax.fori_loop(0, ltiles, streamed, jnp.zeros((rows, LANES), F32))
    sq[plane] = lax.dot_general(
        jnp.ones((8, LANES), F32),
        acc,
        (((1,), (1,)), ((), ())),
        precision=lax.Precision.HIGHEST,
        preferred_element_type=F32,
    )
    for d in range(1, planes):
        to = (plane + d) % planes
        remote(sq.at[plane], sq.at[plane], sq_send, sq_recv, chan=to).start()
    keep_query()

    def far_keys():
        pl.loop(0, early)(far_key)

    drain(sq.at[pl.ds(0, planes - 1)], sq_recv)
    total_sq = sq[0]
    for n in range(1, planes):
        total_sq = total_sq + sq[n]
    width = float(planes * ltiles * LANES)
    scale = lax.rsqrt(total_sq / width + 1e-6).T[:, 0:1]

    def normed(h):
        value = stream[h] * scale * gain_ref[pl.ds(h, 1), :]
        return value.astype(BF16).reshape(rows // TILE, TILE, LANES)

    def send_value(n):
        h = (mine + order(n)) % heads
        vloc[h] = normed(h)
        remote(vloc.at[h], v_all.at[me], v_send, v_recv.at[me], seq=holder_of(h)).start()

    pl.loop(0, VALUES_AHEAD)(send_value)
    vloc[mine] = normed(mine)

    @pl.when(held_here)
    def _():
        pltpu.make_async_copy(vloc.at[mine], v_all.at[me], v_recv.at[me]).start()

    @pl.when(jnp.logical_not(held_here))
    def _():
        remote(
            vloc.at[mine], v_all.at[me], own_sem.at[3], v_recv.at[me], seq=chip_peer
        ).start()

    far_keys()
    keys_arrive()

    @pl.loop(0, heads)
    def _(n):
        drain(rd_all.at[n], rd_recv.at[n])

    to_smem = pltpu.make_async_copy(rd_all, rd_smem, load_sem.at[9])
    to_smem.start()
    to_smem.wait()

    def pick(everything, i, count):
        for j in range(count):
            tiles[j * TILE : (j + 1) * TILE, :] = everything[j, rd_smem[i, 1, j]]

    root = 1.4426950408889634 / float(LANES) ** 0.5
    lanes = (((1,), (1,)), ((), ()))

    def weigh(i, count):
        keys = count * TILE
        query = q_all[i].reshape(rows, LANES)
        shard = my_half * middle + 2 * i + core
        pick(k_all, i, count)
        lane_tile = lax.broadcasted_iota(jnp.int32, (1, LANES), 1) // TILE
        row = lax.broadcasted_iota(jnp.int32, (rows, rows), 0)
        col = lax.broadcasted_iota(jnp.int32, (rows, rows), 1)
        own = lax.dot_general(
            query, k_all[shard].reshape(rows, LANES), lanes, preferred_element_type=F32
        )
        far = lax.dot_general(query, tiles[0:keys, :], lanes, preferred_element_type=F32)
        blocks = [jnp.where(row >= col, own * root, -1e30)]
        zero = jnp.zeros((1, LANES), F32)
        per = LANES // TILE
        for c in range(keys // LANES):
            wanted = jnp.full((1, LANES), -1, jnp.int32)
            for n in range(per):
                wanted = jnp.where(lane_tile == n, rd_smem[i, 0, c * per + n], wanted)
            block = far[:, c * LANES : (c + 1) * LANES] * root
            blocks.append(block + jnp.where(wanted >= 0, zero, -1e30))
        peak = blocks[0]
        for block in blocks[1:]:
            peak = jnp.maximum(peak, block)
        peak = jnp.max(peak, axis=1, keepdims=True)
        total = jnp.zeros((rows, LANES), F32)
        for c, block in enumerate(blocks):
            block = jnp.exp2(block - peak)
            total = total + block
            weights[i, :, c * LANES : (c + 1) * LANES] = block.astype(BF16)
        total = jnp.sum(total, axis=1, keepdims=True)
        totals[i] = jnp.broadcast_to(1.0 / total, (rows, LANES))

    _, share_step, _, arrive = sharing(v_all, v_recv, vf_send)

    @pl.loop(0, heads)
    def _(n):
        drain(q_all.at[n], q_recv.at[n])

        @pl.when(n < heads - 1 - VALUES_AHEAD)
        def _():
            send_value(n + VALUES_AHEAD)

        @pl.when(n >= SHARE_LAG)
        def _():
            share_step(2 * (n - SHARE_LAG))
            share_step(2 * (n - SHARE_LAG) + 1)

        @pl.when(my_half == 0)
        def _():
            weigh(n, middle)

        @pl.when(my_half == 1)
        def _():
            weigh(n, shards)

    pl.loop(2 * (heads - SHARE_LAG), 3 * early)(share_step)
    arrive()

    def attend(i, count):
        keys = count * TILE
        pick(v_all, i, count)
        shard = my_half * middle + 2 * i + core
        summed = jnp.dot(
            weights[i, :, LANES : LANES + keys], tiles[0:keys, :], preferred_element_type=F32
        )
        summed += jnp.dot(
            weights[i, :, 0:LANES],
            v_all[shard].reshape(rows, LANES),
            preferred_element_type=F32,
        )
        o_stage[i] = (summed * totals[i]).astype(BF16)

    @pl.loop(0, heads)
    def _(n):
        i = (mine + 5 * n) % heads
        shard = my_half * middle + 2 * i + core

        @pl.when(my_half == 0)
        def _():
            attend(i, middle)

        @pl.when(my_half == 1)
        def _():
            attend(i, shards)

        @pl.when(shard != me)
        def _():
            remote(
                o_stage.at[i], o_recv.at[mine], o_send.at[i], o_recv_sem.at[mine], seq=shard
            ).start()

        @pl.when(shard == me)
        def _():
            pltpu.make_async_copy(o_stage.at[i], o_recv.at[mine], o_recv_sem.at[mine]).start()

    @pl.loop(0, heads)
    def _(n):
        h = (my_row + heads - n) % heads
        drain(o_recv.at[h], o_recv_sem.at[h])
        cols = columns(h)
        out_v[:, cols] = (stream[h] + o_recv[h].astype(F32)).astype(BF16)

    written = pltpu.make_async_copy(out_v, out, out_sem)
    written.start()

    drain(ends.at[pl.ds(0, LEVEL - 1)], st_send)
    drain(st_out.at[pl.ds(0, LEVEL - 1)], back_send)
    drain(sq.at[pl.ds(0, planes - 1)], sq_send)
    drain(rd_all.at[pl.ds(0, heads - 1)], rd_send)
    drain(q_all.at[pl.ds(0, heads - 1)], q_send)
    drain(q_all.at[pl.ds(0, heads - 1)], k_send)
    drain(q_all.at[pl.ds(0, heads - 1)], v_send)

    @pl.loop(level_at + 1, levels)
    def _(to):
        drain(level, level_send.at[to])

    @pl.when(jnp.logical_not(held_here))
    def _():
        drain(q_all.at[0], own_sem.at[0])
        drain(q_all.at[0], own_sem.at[3])

    @pl.when(jnp.logical_not(at_home))
    def _():
        drain(q_all.at[0], own_sem.at[1])
        drain(rd_all.at[0], own_sem.at[2])

    for fwd in (kf_send, vf_send):

        @pl.when(my_half == 0)
        def _():
            drain(k_all.at[pl.ds(0, 3 * early)], fwd)

        @pl.when(my_half == 1)
        def _():
            drain(k_all.at[pl.ds(0, 5 * early)], fwd)

    @pl.loop(0, heads)
    def _(i):
        @pl.when(my_half * middle + 2 * i + core != me)
        def _():
            drain(o_stage.at[i], o_send.at[i])

    written.wait()


def local(
    shards,
    planes,
    residual,
    hyena_q,
    hyena_k,
    hyena_v,
    modal_residue,
    decay_rate,
    skip_gain,
    attn_q,
    attn_k,
    norm_gain,
    readers,
):
    rows, features = residual.shape
    modes = modal_residue.shape[1]
    ltiles = features // LANES
    heads = shards // GROUP

    hbm = pl.BlockSpec(memory_space=pl.ANY)
    dma = pltpu.SemaphoreType.DMA
    tiled = (rows // TILE, TILE, features)
    block = (rows // TILE, TILE, LANES)
    share = (modes * ltiles // LEVEL, LANES)
    return pl.pallas_call(
        functools.partial(kernel, shards, planes, modes),
        out_shape=jax.ShapeDtypeStruct((rows, features), BF16),
        in_specs=[hbm] * 11,
        out_specs=hbm,
        scratch_shapes=[
            pltpu.VMEM((modes, features), F32),
            pltpu.VMEM((modes, features), F32),
            pltpu.VMEM((ltiles, LANES), F32),
            pltpu.VMEM((ltiles, LANES), F32),
            pltpu.VMEM((1, shards), jnp.int32),
            pltpu.VMEM((rows, features), BF16),
            pltpu.VMEM((rows, features), BF16),
            pltpu.VMEM((rows, features), BF16),
            pltpu.VMEM((rows, features), BF16),
            pltpu.VMEM((2, ltiles * modes, LANES), F32),
            pltpu.VMEM((modes * ltiles, LANES), F32),
            pltpu.VMEM((modes * ltiles, LANES), F32),
            pltpu.VMEM((modes * ltiles, LANES), F32),
            pltpu.VMEM((ltiles * rows, LANES), F32),
            pltpu.VMEM((ltiles * rows, LANES), F32),
            pltpu.VMEM((LEVEL,) + share, F32),
            pltpu.VMEM((LEVEL,) + share, F32),
            pltpu.VMEM(share, F32),
            pltpu.VMEM((shards // LEVEL,) + share, F32),
            pltpu.VMEM((LEVEL,) + share, F32),
            pltpu.VMEM((LEVEL,) + share, F32),
            pltpu.VMEM((ltiles, rows, LANES), F32),
            pltpu.VMEM((planes, 8, LANES), F32),
            pltpu.VMEM((heads,) + block, BF16),
            pltpu.VMEM((heads,) + block, BF16),
            pltpu.VMEM((shards,) + block, BF16),
            pltpu.VMEM((shards,) + block, BF16),
            pltpu.VMEM((2, LANES), jnp.int32),
            pltpu.VMEM((heads, 2, LANES), jnp.int32),
            pltpu.SMEM((heads, 2, LANES), jnp.int32),
            pltpu.VMEM((shards * TILE, LANES), BF16),
            pltpu.VMEM((heads, rows, shards * TILE + rows), BF16),
            pltpu.VMEM((heads, rows, LANES), F32),
            pltpu.VMEM((heads, rows, LANES), BF16),
            pltpu.VMEM((heads, rows, LANES), BF16),
            pltpu.VMEM((rows, features), BF16),
            dma((10,)),
            dma((4,)),
            dma,
            dma,
            dma((shards // LEVEL,)),
            dma((shards // LEVEL,)),
            dma,
            dma,
            dma,
            dma,
            dma,
            dma((heads,)),
            dma,
            dma((heads,)),
            dma,
            dma((shards,)),
            dma,
            dma((shards,)),
            dma,
            dma,
            dma((heads,)),
            dma((heads,)),
            dma,
        ],
        compiler_params=pltpu.CompilerParams(
            collective_id=0, has_side_effects=True, vmem_limit_bytes=60 * 1024 * 1024
        ),
    )(
        residual,
        hyena_q,
        hyena_k,
        hyena_v,
        modal_residue.T,
        decay_rate.T,
        skip_gain.reshape(ltiles, LANES),
        attn_q.reshape(tiled),
        attn_k.reshape(tiled),
        norm_gain.reshape(ltiles, LANES),
        readers,
    )


def solution(mesh):
    spread = P("seq", "chan")
    placed = (
        spread,
        spread,
        spread,
        spread,
        P("chan", None),
        P("chan", None),
        P("chan"),
        spread,
        spread,
        P("chan"),
        P("seq", None),
    )
    return jax.shard_map(
        functools.partial(local, mesh.shape["seq"], mesh.shape["chan"]),
        mesh=mesh,
        in_specs=placed,
        out_specs=spread,
        check_vma=False,
    )
```

```python
import functools

import jax
import jax.numpy as jnp
from jax import lax
from jax.experimental import pallas as pl
from jax.experimental.pallas import tpu as pltpu
from jax.sharding import PartitionSpec as P

MESH = pl.DeviceIdType.MESH
LANES = 128
TILE = 16
GROUP = 4
LEVEL = 8
SHARE_LAG = 4
VALUES_AHEAD = 15
BLOCKS_AT = (4, 1, 4, 6, 6)
F32 = jnp.float32
BF16 = jnp.bfloat16


def remote(src, dst, send, recv, **where):
    return pltpu.make_async_remote_copy(
        src_ref=src,
        dst_ref=dst,
        send_sem=send,
        recv_sem=recv,
        device_id=where,
        device_id_type=MESH,
    )


def drain(ref, sem):
    pltpu.make_async_copy(ref, ref, sem).wait()


def kernel(
    shards,
    planes,
    modes,
    residual,
    hyena_q,
    hyena_k,
    hyena_v,
    residue_hbm,
    rate_hbm,
    skip_hbm,
    attn_q,
    attn_k,
    gain_hbm,
    readers_hbm,
    out,
    residue_ref,
    rate_ref,
    skip_ref,
    gain_ref,
    readers,
    hk,
    hv,
    hq,
    res,
    by_tile,
    rates,
    residues,
    decay,
    xs,
    ys,
    ends,
    st_in,
    level,
    level_in,
    st_out,
    start,
    stream,
    sq,
    vloc,
    q_all,
    k_all,
    v_all,
    rd_mine,
    rd_all,
    rd_smem,
    tiles,
    weights,
    totals,
    o_stage,
    o_recv,
    out_v,
    load_sem,
    own_sem,
    st_send,
    st_recv,
    level_send,
    level_recv,
    back_send,
    back_recv,
    sq_send,
    sq_recv,
    rd_send,
    rd_recv,
    q_send,
    q_recv,
    k_send,
    k_recv,
    v_send,
    v_recv,
    kf_send,
    vf_send,
    o_send,
    o_recv_sem,
    out_sem,
):
    me = lax.axis_index("seq")
    plane = lax.axis_index("chan")
    heads = shards // GROUP
    mine = me // GROUP
    core = me % 2
    side = (me // 2) % 2
    core_peer = me + 1 - 2 * core
    chip_peer = me + 2 - 4 * side
    middle = shards // 2
    half = me // middle
    turned = (mine // 2) % 2
    my_half = (side + turned) % 2
    my_row = (me % middle) // 2
    place = me % LEVEL
    level_at = me // LEVEL
    levels = shards // LEVEL
    rows = hk.shape[0]
    ltiles = hk.shape[1] // LANES

    loads = [
        pltpu.make_async_copy(src, dst, load_sem.at[n])
        for n, (src, dst) in enumerate(
            (
                (hyena_k, hk),
                (hyena_v, hv),
                (rate_hbm, rate_ref),
                (residue_hbm, residue_ref),
                (readers_hbm, readers),
                (skip_hbm, skip_ref),
                (gain_hbm, gain_ref),
                (hyena_q, hq),
                (residual, res),
            )
        )
    ]
    for load in loads:
        load.start()

    barrier = pltpu.get_barrier_semaphore()

    @pl.loop(0, LEVEL // 2)
    def _(n):
        to = level_at * LEVEL + 2 * n + 1 - core
        pl.semaphore_signal(barrier, inc=1, device_id={"seq": to}, device_id_type=MESH)

    for d in range(1, planes):
        to = (plane + d) % planes
        pl.semaphore_signal(barrier, inc=1, device_id={"chan": to}, device_id_type=MESH)

    @pl.loop(1, middle)
    def _(d):
        to = (me + 2 * d) % shards
        pl.semaphore_signal(barrier, inc=1, device_id={"seq": to}, device_id_type=MESH)

    def order(n):
        return heads // 2 + (1 - n % 2) * (n // 2) - (n % 2) * ((n + 1) // 2)

    def columns(h):
        return pl.ds(pl.multiple_of(h * LANES, LANES), LANES)

    def reader_of(h):
        return h * GROUP + 2 * ((half + h // 2) % 2) + core

    def holder_of(h):
        return h * GROUP + 2 * (half * ((1 + h // 2) % 2) + (1 - half) * side) + core

    at_home = half == my_half
    held_here = jnp.logical_or(half == 0, at_home)

    def send_keys(low, high):
        @pl.loop(low, high)
        def _(n):
            send_key(n)

    def send_key(n):
        h = (mine + order(n)) % heads
        remote(
            attn_k.at[:, :, columns(h)], k_all.at[me], k_send, k_recv.at[me], seq=holder_of(h)
        ).start()

    def send_query(n):
        h = (mine + order(n)) % heads
        to = reader_of(h)
        remote(rd_mine, rd_all.at[my_row], rd_send, rd_recv.at[my_row], seq=to).start()
        remote(
            attn_q.at[:, :, columns(h)], q_all.at[my_row], q_send, q_recv.at[my_row], seq=to
        ).start()

    def send_queries(low, high):
        @pl.loop(low, high)
        def _(n):
            send_query(n)

    def send_blocks(low, high):
        split = heads - 1
        if low < min(high, split):
            send_keys(low, min(high, split))
        if max(low, split) < high:
            send_queries(max(low, split) - split, high - split)

    def keep_key():
        @pl.when(held_here)
        def _():
            pltpu.make_async_copy(
                attn_k.at[:, :, columns(mine)], k_all.at[me], k_recv.at[me]
            ).start()

        @pl.when(jnp.logical_not(held_here))
        def _():
            remote(
                attn_k.at[:, :, columns(mine)],
                k_all.at[me],
                own_sem.at[0],
                k_recv.at[me],
                seq=chip_peer,
            ).start()

    def keep_query():
        @pl.when(at_home)
        def _():
            pltpu.make_async_copy(
                attn_q.at[:, :, columns(mine)], q_all.at[my_row], q_recv.at[my_row]
            ).start()
            pltpu.make_async_copy(rd_mine, rd_all.at[my_row], rd_recv.at[my_row]).start()

        @pl.when(jnp.logical_not(at_home))
        def _():
            remote(
                attn_q.at[:, :, columns(mine)],
                q_all.at[my_row],
                own_sem.at[1],
                q_recv.at[my_row],
                seq=chip_peer,
            ).start()
            remote(
                rd_mine, rd_all.at[my_row], own_sem.at[2], rd_recv.at[my_row], seq=chip_peer
            ).start()

    pl.semaphore_wait(barrier, LEVEL // 2 + planes - 1 + middle - 1)
    at_entry, at_stretch, at_share, at_level, at_back = BLOCKS_AT
    keep_key()
    send_blocks(0, at_entry)
    issued = at_entry

    loads[2].wait()
    loads[3].wait()
    loads[4].wait()

    def spread_modes(lt, _):
        cols = pl.ds(pl.multiple_of(lt * LANES, LANES), LANES)
        at = pl.ds(pl.multiple_of(lt * modes, modes), modes)
        by_tile[0, at, :] = rate_ref[:, cols]
        by_tile[1, at, :] = residue_ref[:, cols]
        return _

    lax.fori_loop(0, ltiles, spread_modes, 0)
    for m in range(modes):
        for part in range(ltiles // 8):
            of_mode = pl.ds(part * 8 * modes + m, 8, stride=modes)
            sub = slice(m * ltiles + part * 8, m * ltiles + part * 8 + 8)
            rate = by_tile[0, of_mode, :]
            rates[sub, :] = rate
            decay[sub, :] = jnp.exp(-rate)
            residues[sub, :] = by_tile[1, of_mode, :]
    wanted = readers[...]
    rd_mine[...] = jnp.zeros_like(rd_mine)
    rd_mine[0:1, 0:shards] = wanted
    rd_mine[1:2, 0:shards] = jnp.maximum(wanted, 0)
    loads[0].wait()
    loads[1].wait()

    @pl.loop(0, ltiles)
    def _(lt):
        cols = pl.ds(pl.multiple_of(lt * LANES, LANES), LANES)
        product = (hk[:, cols].astype(F32) * hv[:, cols].astype(F32)).astype(BF16)
        xs[pl.ds(pl.multiple_of(lt * rows, rows), rows), :] = product.astype(F32)

    per_place = modes // LEVEL
    parts = ltiles // 8

    def mode_rows(m, part):
        return slice(m * ltiles + part * 8, m * ltiles + part * 8 + 8)

    def share_rows(m, part):
        at = (m % per_place) * ltiles + part * 8
        return slice(at, at + 8)

    for part in range(parts):
        base = part * 8 * rows

        def advance(t, states):
            x = xs[pl.ds(base + t, 8, stride=rows), :]
            return tuple(decay[mode_rows(m, part), :] * states[m] + x for m in range(modes))

        def stretch(n, states, part=part, advance=advance):
            if at_stretch:
                send_key(at_entry + part * 2 + n)
            span = rows // 2

            def inner(t, states):
                return advance(n * span + t, states)

            return lax.fori_loop(0, span, inner, states, unroll=4)

        states = lax.fori_loop(
            0, 2, stretch, tuple(jnp.zeros((8, LANES), F32) for _ in range(modes))
        )
        for m in range(modes):
            ends[m // per_place, share_rows(m, part), :] = states[m]

    issued += 2 * parts * at_stretch

    @pl.loop(1, LEVEL)
    def _(d):
        at = (place + d) % LEVEL
        to = level_at * LEVEL + at
        remote(ends.at[at], st_in.at[place], st_send, st_recv, seq=to).start()

    st_in[place] = ends[place]
    send_blocks(issued, issued + at_share)
    issued += at_share

    my_rates = rates[pl.ds(pl.multiple_of(place * per_place * ltiles, 8), per_place * ltiles), :]
    across = jnp.exp(-float(rows) * my_rates)
    across_level = jnp.exp(-float(rows * LEVEL) * my_rates)
    drain(st_in.at[pl.ds(0, LEVEL - 1)], st_recv)
    carry = st_in[0]
    for n in range(1, LEVEL):
        carry = across * carry + st_in[n]
    level[...] = carry

    @pl.loop(level_at + 1, levels)
    def _(to):
        remote(
            level,
            level_in.at[level_at],
            level_send.at[to],
            level_recv.at[level_at],
            seq=to * LEVEL + place,
        ).start()

    send_blocks(issued, issued + at_level)
    issued += at_level

    def before(n, carry):
        drain(level_in.at[n], level_recv.at[n])
        return across_level * carry + level_in[n]

    carry = lax.fori_loop(0, level_at, before, jnp.zeros_like(carry))
    for n in range(LEVEL):
        st_out[n] = carry
        carry = across * carry + st_in[n]

    @pl.loop(1, LEVEL)
    def _(d):
        at = (place + d) % LEVEL
        to = level_at * LEVEL + at
        remote(st_out.at[at], start.at[place], back_send, back_recv, seq=to).start()

    start[place] = st_out[place]
    send_blocks(issued, issued + at_back)
    issued += at_back
    loads[5].wait()
    loads[6].wait()
    loads[7].wait()
    loads[8].wait()
    drain(start.at[pl.ds(0, LEVEL - 1)], back_recv)

    early = heads // 2

    def sharing(everything, recv, fwd):
        def pass_on(slot, to):
            remote(everything.at[slot], everything.at[slot], fwd, recv.at[slot], seq=to).start()

        def share_slot(slot, to_chip):
            drain(everything.at[slot], recv.at[slot])
            if to_chip:
                pass_on(slot, chip_peer)
            pass_on(slot, core_peer)

        def share_far(n):
            slot = n * GROUP + 2 * (1 - side) + core
            share_slot(slot, False)

        def share_from(n):
            group = (mine + heads - order(n)) % heads

            @pl.when(group < early)
            def _():
                share_slot(group * GROUP + 2 * side + core, True)

            @pl.when(jnp.logical_and(group >= early, my_half == 1))
            def _():
                share_slot(group * GROUP + core, False)
                share_slot(group * GROUP + 2 + core, False)

        def share_step(k):
            near = (k + mine) % early

            @pl.when(k < early)
            def _():
                share_slot(near * GROUP + 2 * side + core, True)

            @pl.when(jnp.logical_and(k >= early, k < 2 * early))
            def _():
                share_far(near)

            @pl.when(jnp.logical_and(k >= 2 * early, my_half == 1))
            def _():
                share_slot((early + near) * GROUP + core, False)
                share_slot((early + near) * GROUP + 2 + core, False)

        def arrive():
            @pl.loop(0, middle // 2)
            def _(n):
                slot = 2 * n + 1 - core
                drain(everything.at[slot], recv.at[slot])

            @pl.when(my_half == 1)
            def _():
                @pl.loop(middle // 2, middle)
                def _(n):
                    slot = 2 * n + 1 - core
                    drain(everything.at[slot], recv.at[slot])

        return share_from, share_step, share_far, arrive

    key_from, _, far_key, keys_arrive = sharing(k_all, k_recv, kf_send)
    for part in range(parts):
        base = part * 8 * rows
        skip = skip_ref[part * 8 : part * 8 + 8, :]

        def filtered(t, states):
            x = xs[pl.ds(base + t, 8, stride=rows), :]
            states = tuple(decay[mode_rows(m, part), :] * states[m] + x for m in range(modes))
            terms = [residues[mode_rows(m, part), :] * states[m] for m in range(modes)]
            terms.append(skip * x)
            while len(terms) > 1:
                paired = [terms[n] + terms[n + 1] for n in range(0, len(terms) - 1, 2)]
                terms = paired + terms[len(paired) * 2 :]
            ys[pl.ds(base + t, 8, stride=rows), :] = terms[0]
            return states

        first = tuple(start[m // per_place, share_rows(m, part), :] for m in range(modes))

        lax.fori_loop(0, rows, filtered, first, unroll=4)
        steps = heads // parts
        pl.loop(part * steps, (part + 1) * steps)(key_from)
        left = 2 * (heads - 1) - issued
        send_blocks(issued + left * part // parts, issued + left * (part + 1) // parts)

    def streamed(lt, acc):
        cols = columns(lt)
        convolved = ys[pl.ds(pl.multiple_of(lt * rows, rows), rows), :].astype(BF16).astype(F32)
        value = res[:, cols].astype(F32) + hq[:, cols].astype(F32) * convolved
        stream[lt] = value
        return acc + value * value

    acc = lax.fori_loop(0, ltiles, streamed, jnp.zeros((rows, LANES), F32))
    sq[plane] = lax.dot_general(
        jnp.ones((8, LANES), F32),
        acc,
        (((1,), (1,)), ((), ())),
        precision=lax.Precision.HIGHEST,
        preferred_element_type=F32,
    )
    for d in range(1, planes):
        to = (plane + d) % planes
        remote(sq.at[plane], sq.at[plane], sq_send, sq_recv, chan=to).start()
    keep_query()

    def far_keys():
        pl.loop(0, early)(far_key)

    drain(sq.at[pl.ds(0, planes - 1)], sq_recv)
    total_sq = sq[0]
    for n in range(1, planes):
        total_sq = total_sq + sq[n]
    width = float(planes * ltiles * LANES)
    scale = lax.rsqrt(total_sq / width + 1e-6).T[:, 0:1]

    def normed(h):
        value = stream[h] * scale * gain_ref[pl.ds(h, 1), :]
        return value.astype(BF16).reshape(rows // TILE, TILE, LANES)

    def send_value(n):
        h = (mine + order(n)) % heads
        vloc[h] = normed(h)
        remote(vloc.at[h], v_all.at[me], v_send, v_recv.at[me], seq=holder_of(h)).start()

    pl.loop(0, VALUES_AHEAD)(send_value)
    vloc[mine] = normed(mine)

    @pl.when(held_here)
    def _():
        pltpu.make_async_copy(vloc.at[mine], v_all.at[me], v_recv.at[me]).start()

    @pl.when(jnp.logical_not(held_here))
    def _():
        remote(
            vloc.at[mine], v_all.at[me], own_sem.at[3], v_recv.at[me], seq=chip_peer
        ).start()

    far_keys()
    keys_arrive()

    @pl.loop(0, heads)
    def _(n):
        drain(rd_all.at[n], rd_recv.at[n])

    to_smem = pltpu.make_async_copy(rd_all, rd_smem, load_sem.at[9])
    to_smem.start()
    to_smem.wait()

    def pick(everything, i, count):
        for j in range(count):
            tiles[j * TILE : (j + 1) * TILE, :] = everything[j, rd_smem[i, 1, j]]

    root = 1.4426950408889634 / float(LANES) ** 0.5
    lanes = (((1,), (1,)), ((), ()))

    def weigh(i, count):
        keys = count * TILE
        query = q_all[i].reshape(rows, LANES)
        shard = my_half * middle + 2 * i + core
        pick(k_all, i, count)
        lane_tile = lax.broadcasted_iota(jnp.int32, (1, LANES), 1) // TILE
        row = lax.broadcasted_iota(jnp.int32, (rows, rows), 0)
        col = lax.broadcasted_iota(jnp.int32, (rows, rows), 1)
        own = lax.dot_general(
            query, k_all[shard].reshape(rows, LANES), lanes, preferred_element_type=F32
        )
        far = lax.dot_general(query, tiles[0:keys, :], lanes, preferred_element_type=F32)
        blocks = [jnp.where(row >= col, own * root, -1e30)]
        zero = jnp.zeros((1, LANES), F32)
        per = LANES // TILE
        for c in range(keys // LANES):
            wanted = jnp.full((1, LANES), -1, jnp.int32)
            for n in range(per):
                wanted = jnp.where(lane_tile == n, rd_smem[i, 0, c * per + n], wanted)
            block = far[:, c * LANES : (c + 1) * LANES] * root
            blocks.append(block + jnp.where(wanted >= 0, zero, -1e30))
        peak = blocks[0]
        for block in blocks[1:]:
            peak = jnp.maximum(peak, block)
        peak = jnp.max(peak, axis=1, keepdims=True)
        total = jnp.zeros((rows, LANES), F32)
        for c, block in enumerate(blocks):
            block = jnp.exp2(block - peak)
            total = total + block
            weights[i, :, c * LANES : (c + 1) * LANES] = block.astype(BF16)
        total = jnp.sum(total, axis=1, keepdims=True)
        totals[i] = jnp.broadcast_to(1.0 / total, (rows, LANES))

    _, share_step, _, arrive = sharing(v_all, v_recv, vf_send)

    @pl.loop(0, heads)
    def _(n):
        drain(q_all.at[n], q_recv.at[n])

        @pl.when(n < heads - 1 - VALUES_AHEAD)
        def _():
            send_value(n + VALUES_AHEAD)

        @pl.when(n >= SHARE_LAG)
        def _():
            share_step(2 * (n - SHARE_LAG))
            share_step(2 * (n - SHARE_LAG) + 1)

        @pl.when(my_half == 0)
        def _():
            weigh(n, middle)

        @pl.when(my_half == 1)
        def _():
            weigh(n, shards)

    pl.loop(2 * (heads - SHARE_LAG), 3 * early)(share_step)
    arrive()

    def attend(i, count):
        keys = count * TILE
        pick(v_all, i, count)
        shard = my_half * middle + 2 * i + core
        summed = jnp.dot(
            weights[i, :, LANES : LANES + keys], tiles[0:keys, :], preferred_element_type=F32
        )
        summed += jnp.dot(
            weights[i, :, 0:LANES],
            v_all[shard].reshape(rows, LANES),
            preferred_element_type=F32,
        )
        o_stage[i] = (summed * totals[i]).astype(BF16)

    @pl.loop(0, heads)
    def _(n):
        i = (mine + 5 * n) % heads
        shard = my_half * middle + 2 * i + core

        @pl.when(my_half == 0)
        def _():
            attend(i, middle)

        @pl.when(my_half == 1)
        def _():
            attend(i, shards)

        @pl.when(shard != me)
        def _():
            remote(
                o_stage.at[i], o_recv.at[mine], o_send.at[i], o_recv_sem.at[mine], seq=shard
            ).start()

        @pl.when(shard == me)
        def _():
            pltpu.make_async_copy(o_stage.at[i], o_recv.at[mine], o_recv_sem.at[mine]).start()

    @pl.loop(0, heads)
    def _(n):
        h = (my_row + heads - n) % heads
        drain(o_recv.at[h], o_recv_sem.at[h])
        cols = columns(h)
        out_v[:, cols] = (stream[h] + o_recv[h].astype(F32)).astype(BF16)
        pltpu.make_async_copy(out_v.at[:, cols], out.at[:, cols], out_sem).start()


    drain(ends.at[pl.ds(0, LEVEL - 1)], st_send)
    drain(st_out.at[pl.ds(0, LEVEL - 1)], back_send)
    drain(sq.at[pl.ds(0, planes - 1)], sq_send)
    drain(rd_all.at[pl.ds(0, heads - 1)], rd_send)
    drain(q_all.at[pl.ds(0, heads - 1)], q_send)
    drain(q_all.at[pl.ds(0, heads - 1)], k_send)
    drain(q_all.at[pl.ds(0, heads - 1)], v_send)

    @pl.loop(level_at + 1, levels)
    def _(to):
        drain(level, level_send.at[to])

    @pl.when(jnp.logical_not(held_here))
    def _():
        drain(q_all.at[0], own_sem.at[0])
        drain(q_all.at[0], own_sem.at[3])

    @pl.when(jnp.logical_not(at_home))
    def _():
        drain(q_all.at[0], own_sem.at[1])
        drain(rd_all.at[0], own_sem.at[2])

    for fwd in (kf_send, vf_send):

        @pl.when(my_half == 0)
        def _():
            drain(k_all.at[pl.ds(0, 3 * early)], fwd)

        @pl.when(my_half == 1)
        def _():
            drain(k_all.at[pl.ds(0, 5 * early)], fwd)

    @pl.loop(0, heads)
    def _(i):
        @pl.when(my_half * middle + 2 * i + core != me)
        def _():
            drain(o_stage.at[i], o_send.at[i])

    drain(out_v, out_sem)


def local(
    shards,
    planes,
    residual,
    hyena_q,
    hyena_k,
    hyena_v,
    modal_residue,
    decay_rate,
    skip_gain,
    attn_q,
    attn_k,
    norm_gain,
    readers,
):
    rows, features = residual.shape
    modes = modal_residue.shape[1]
    ltiles = features // LANES
    heads = shards // GROUP

    hbm = pl.BlockSpec(memory_space=pl.ANY)
    dma = pltpu.SemaphoreType.DMA
    tiled = (rows // TILE, TILE, features)
    block = (rows // TILE, TILE, LANES)
    share = (modes * ltiles // LEVEL, LANES)
    return pl.pallas_call(
        functools.partial(kernel, shards, planes, modes),
        out_shape=jax.ShapeDtypeStruct((rows, features), BF16),
        in_specs=[hbm] * 11,
        out_specs=hbm,
        scratch_shapes=[
            pltpu.VMEM((modes, features), F32),
            pltpu.VMEM((modes, features), F32),
            pltpu.VMEM((ltiles, LANES), F32),
            pltpu.VMEM((ltiles, LANES), F32),
            pltpu.VMEM((1, shards), jnp.int32),
            pltpu.VMEM((rows, features), BF16),
            pltpu.VMEM((rows, features), BF16),
            pltpu.VMEM((rows, features), BF16),
            pltpu.VMEM((rows, features), BF16),
            pltpu.VMEM((2, ltiles * modes, LANES), F32),
            pltpu.VMEM((modes * ltiles, LANES), F32),
            pltpu.VMEM((modes * ltiles, LANES), F32),
            pltpu.VMEM((modes * ltiles, LANES), F32),
            pltpu.VMEM((ltiles * rows, LANES), F32),
            pltpu.VMEM((ltiles * rows, LANES), F32),
            pltpu.VMEM((LEVEL,) + share, F32),
            pltpu.VMEM((LEVEL,) + share, F32),
            pltpu.VMEM(share, F32),
            pltpu.VMEM((shards // LEVEL,) + share, F32),
            pltpu.VMEM((LEVEL,) + share, F32),
            pltpu.VMEM((LEVEL,) + share, F32),
            pltpu.VMEM((ltiles, rows, LANES), F32),
            pltpu.VMEM((planes, 8, LANES), F32),
            pltpu.VMEM((heads,) + block, BF16),
            pltpu.VMEM((heads,) + block, BF16),
            pltpu.VMEM((shards,) + block, BF16),
            pltpu.VMEM((shards,) + block, BF16),
            pltpu.VMEM((2, LANES), jnp.int32),
            pltpu.VMEM((heads, 2, LANES), jnp.int32),
            pltpu.SMEM((heads, 2, LANES), jnp.int32),
            pltpu.VMEM((shards * TILE, LANES), BF16),
            pltpu.VMEM((heads, rows, shards * TILE + rows), BF16),
            pltpu.VMEM((heads, rows, LANES), F32),
            pltpu.VMEM((heads, rows, LANES), BF16),
            pltpu.VMEM((heads, rows, LANES), BF16),
            pltpu.VMEM((rows, features), BF16),
            dma((10,)),
            dma((4,)),
            dma,
            dma,
            dma((shards // LEVEL,)),
            dma((shards // LEVEL,)),
            dma,
            dma,
            dma,
            dma,
            dma,
            dma((heads,)),
            dma,
            dma((heads,)),
            dma,
            dma((shards,)),
            dma,
            dma((shards,)),
            dma,
            dma,
            dma((heads,)),
            dma((heads,)),
            dma,
        ],
        compiler_params=pltpu.CompilerParams(
            collective_id=0, has_side_effects=True, vmem_limit_bytes=60 * 1024 * 1024
        ),
    )(
        residual,
        hyena_q,
        hyena_k,
        hyena_v,
        modal_residue.T,
        decay_rate.T,
        skip_gain.reshape(ltiles, LANES),
        attn_q.reshape(tiled),
        attn_k.reshape(tiled),
        norm_gain.reshape(ltiles, LANES),
        readers,
    )


def solution(mesh):
    spread = P("seq", "chan")
    placed = (
        spread,
        spread,
        spread,
        spread,
        P("chan", None),
        P("chan", None),
        P("chan"),
        spread,
        spread,
        P("chan"),
        P("seq", None),
    )
    return jax.shard_map(
        functools.partial(local, mesh.shape["seq"], mesh.shape["chan"]),
        mesh=mesh,
        in_specs=placed,
        out_specs=spread,
        check_vma=False,
    )
```
